128 devices in a mesh: segment: 2 (over z_hi), dp: 32 (over y, x, core), rows: 2 (over z_lo).
Axes of the slice: x: 4, y: 4, z: 4 (z_hi: 2, z_lo: 2; z = z_hi * 2 + z_lo), core: 2. Of those that a mesh axis runs over, the one named last changes fastest.
Arguments:
- segment_inputs: bfloat16 [2, 64, 32, 32, 640], P('segment', 'dp', 'rows'), may hold values from -6 to 6
- weights: bfloat16 [2, 9, 640, 640], P('segment', None, 'dp'), may hold values from -0.078125 to 0.078125
- gains: float32 [2, 640], P('segment'), may hold values from 0.5 to 1.5
- shifts: float32 [2, 640], P('segment'), may hold values from -3 to 3
- chain_cot: bfloat16 [64, 32, 32, 640], P('dp', 'rows'), may hold values from -6 to 6
- skip_cot: bfloat16 [64, 32, 32, 640], P('dp', 'rows'), may hold values from -6 to 6
Outputs:
- input_grads: bfloat16 [2, 64, 32, 32, 640], P('segment', 'dp', 'rows')
- weight_grads: float32 [2, 9, 640, 640], P('segment', None, 'dp')
- gain_grads: float32 [2, 640], P('segment')
- shift_grads: float32 [2, 640], P('segment')
The draws below stay inside these ranges and needn't reach their ends.
All inputs are finite; a program needn't handle non-finite values.
Results may differ from the reference program's by a relative error of at most 0.0014.
The reference program's roundings to bfloat16 on the way (of `active`, `shifted` and `handed`) count: a program that leaves them out, or rounds other values in their place, can miss the bound.
Values may be sent and summed in bfloat16 or wider, within the bound.
No kernel may reach another device: no remote copies, remote signals or barrier semaphores. Data moves between devices by JAX's collectives and lax.ppermute only.
A program may use at most 128 MiB of HBM per device.

```python
import jax
import jax.numpy as jnp
from jax import lax

CHANNELS = 640
GROUPS = 16
HEIGHT = 32
COLUMNS = 32
BATCH = 64


def with_spikes(drawn, rng, source, target, shards_of, factor):
    owner, partner = [(jnp.arange(drawn.shape[axis_at]) // (drawn.shape[axis_at] // shards_of)).reshape([-1 if axis == axis_at else 1 for axis in range(drawn.ndim)]) for axis_at in (source, target)]
    chosen = jax.random.permutation(rng, shards_of)[partner]
    strong = (owner == chosen) | (owner == (partner + shards_of // 2) % shards_of)
    return jnp.where(strong, factor * drawn, drawn)


def levels(key, dims, pieces, low, high):
    def one(axis_at, blocks):
        heights = jax.random.uniform(jax.random.fold_in(jax.random.fold_in(key, 6), axis_at), (blocks,), jnp.float32, low / len(pieces), high / len(pieces))
        return jnp.repeat(jnp.exp(heights), dims[axis_at] // blocks).reshape((-1,) + (1,) * (len(dims) - axis_at - 1))

    factor_of = one(*pieces[0])
    for cut in pieces[1:]:
        factor_of = factor_of * one(*cut)
    return factor_of


def gaussian(stream_key, dims, scale, limit, split=(), kind=jnp.bfloat16):
    result = scale * jax.random.normal(stream_key, dims, jnp.float32)
    if split:
        result = result * levels(stream_key, dims, split, -0.22, 0.18)
    return jnp.clip(result, -limit, limit).astype(kind)


def bell_draw_with(stream_key, extent, spread, limit, split, heavy, dtype=jnp.bfloat16):
    entries = spread * jax.random.normal(stream_key, extent, jnp.float32)
    if split:
        entries = entries * levels(stream_key, extent, split, -0.22, 0.18)
    return jnp.clip(with_spikes(entries, jax.random.fold_in(stream_key, 3), *heavy), -limit, limit).astype(dtype)


def setup_inputs(seed: int = 0) -> dict:
    arg_keys = jax.random.split(jax.random.key(seed), 7)
    return {
        "segment_inputs": bell_draw_with(arg_keys[0], (2, BATCH, HEIGHT, COLUMNS, CHANNELS), 1.0, 6.0, ((0, 2), (1, 32), (2, 2)), (1, 4, 32, 2.75)),
        "weights": gaussian(arg_keys[1], (2, 9, CHANNELS, CHANNELS), (9 * CHANNELS) ** -0.5, 0.078125, ((0, 2), (2, 32))),
        "gains": jnp.clip(1.0 + 0.1 * jax.random.normal(arg_keys[2], (2, CHANNELS), jnp.float32), 0.5, 1.5),
        "shifts": gaussian(arg_keys[3], (2, CHANNELS), 0.5, 3.0, ((0, 2),), jnp.float32),
        "chain_cot": gaussian(arg_keys[4], (BATCH, HEIGHT, COLUMNS, CHANNELS), 1.0, 6.0, ((0, 32), (1, 2))),
        "skip_cot": gaussian(arg_keys[5], (BATCH, HEIGHT, COLUMNS, CHANNELS), 1.0, 6.0, ((0, 32), (1, 2))),
    }


epsilon = 1e-05
offsets = [(-1, -1), (-1, 0), (-1, 1), (0, -1), (0, 0), (0, 1), (1, -1), (1, 0), (1, 1)]

def stencil(padded, height, columns):
    return jnp.stack([padded[1 - row_off:1 - row_off + height, 1 - col_off:1 - col_off + columns] for row_off, col_off in offsets], axis=2)

def segment_back(inputs, adjoint, weight, gain, shift, count_all):
    height, columns, channels = inputs.shape
    per_group = channels // GROUPS
    pixels = height * columns
    grouped = inputs.reshape(pixels, GROUPS, per_group)
    group_mean = lax.optimization_barrier(jnp.sum(grouped, axis=(0, 2))) / count_all
    squares = lax.optimization_barrier(jnp.sum(grouped * grouped, axis=(0, 2))) / count_all
    inv_std = lax.rsqrt(squares - group_mean * group_mean + epsilon)
    normed = ((grouped - group_mean[None, :, None]) * inv_std[None, :, None]).reshape(pixels, channels)
    preact = normed * gain + shift
    gate_val = jax.nn.sigmoid(preact)
    active = (preact * gate_val).astype(jnp.bfloat16)
    padded = jnp.pad(adjoint, ((1, 1), (1, 1), (0, 0)))
    shifted = stencil(padded, height, columns).reshape(pixels, 9, channels)
    back_prop = jnp.einsum('pko,kio->pi', shifted.astype(jnp.float32), weight.astype(jnp.float32))
    weight_grad = jnp.einsum('pi,pko->kio', active.astype(jnp.float32), shifted.astype(jnp.float32))
    pre_grad = back_prop * (gate_val * (1.0 + preact * (1.0 - gate_val)))
    gain_grad = lax.optimization_barrier(jnp.sum(pre_grad * normed, axis=0))
    shift_grad = lax.optimization_barrier(jnp.sum(pre_grad, axis=0))
    norm_grad = (pre_grad * gain).reshape(pixels, GROUPS, per_group)
    norm_group = normed.reshape(pixels, GROUPS, per_group)
    first_sum = lax.optimization_barrier(jnp.sum(norm_grad, axis=(0, 2))) / count_all
    second = lax.optimization_barrier(jnp.sum(norm_grad * norm_group, axis=(0, 2))) / count_all
    in_grad = inv_std[None, :, None] * (norm_grad - first_sum[None, :, None] - norm_group * second[None, :, None])
    return (in_grad.reshape(height, columns, channels), weight_grad, gain_grad, shift_grad)

def reference(segment_inputs, weights, gains, shifts, chain_cot, skip_cot):
    height, columns, channels = segment_inputs.shape[2:]
    count_all = float(height * columns * (channels // GROUPS))

    def per_sample(carry, sliced):
        first_in, second_in, chain_one, skip_one = sliced
        outside = chain_one.astype(jnp.float32) + skip_one.astype(jnp.float32)
        grad_one, wgt_one, gain_one, shift_one = segment_back(second_in.astype(jnp.float32), outside.astype(jnp.bfloat16), weights[1], gains[1], shifts[1], count_all)
        handed = grad_one.astype(jnp.bfloat16)
        grad_zero, wgt_zero, gain_zero, shift_zero = segment_back(first_in.astype(jnp.float32), handed, weights[0], gains[0], shifts[0], count_all)
        block_grad = (outside + grad_zero).astype(jnp.bfloat16)
        new_carry = (carry[0] + wgt_zero, carry[1] + wgt_one, carry[2] + gain_zero, carry[3] + gain_one, carry[4] + shift_zero, carry[5] + shift_one)
        return (new_carry, (block_grad, handed))
    zero_w = jnp.zeros((9, channels, channels), jnp.float32)
    zero_c = jnp.zeros((channels,), jnp.float32)
    carry, grads = lax.scan(per_sample, (zero_w, zero_w, zero_c, zero_c, zero_c, zero_c), (segment_inputs[0], segment_inputs[1], chain_cot, skip_cot))
    input_grads = jnp.stack([grads[0], grads[1]])
    weight_grads = jnp.stack([carry[0], carry[1]])
    gain_grads = jnp.stack([carry[2], carry[3]])
    shift_grads = jnp.stack([carry[4], carry[5]])
    return (input_grads, weight_grads, gain_grads, shift_grads)
```

```python
import jax
import jax.numpy as jnp
import numpy as np
from jax import lax
from jax.experimental import pallas as pl
from jax.experimental.pallas import tpu as pltpu
from jax.sharding import PartitionSpec as P

GROUPS = 16
epsilon = 1e-05
F32 = jnp.float32
BF16 = jnp.bfloat16

CH = 640
PX = 1024
HALF = 512
COLS = 32
LOCAL = 160
SHARD = 10
TAPS = [(-1, -1), (-1, 0), (-1, 1), (0, -1), (0, 0), (0, 1), (1, -1), (1, 0), (1, 1)]

AX, BX, AY, BY = 1, 3, 4, 12
ORDERS = [(AX, BX, AY, BY), (BX, AX, BY, AY), (AY, BY, AX, BX), (BY, AY, BX, AX)]
GATHER_PARTS = [((0, 1, 2, 3, 4), 0), ((5, 6, 7, 8), 2)]
SCATTER_PARTS = [((0, 3), 0), ((1, 4), 1), ((2, 5), 2), ((6, 7, 8), 3)]

VMEM = 58 * 1024 * 1024


def slot_masks(order):
    return [
        (u >> 3 & 1) * order[0] ^ (u >> 2 & 1) * order[1] ^ (u >> 1 & 1) * order[2] ^ (u & 1) * order[3]
        for u in range(16)
    ]


def reorder(order):
    here, base = slot_masks(ORDERS[order]), slot_masks(ORDERS[0])
    out = np.zeros((LOCAL, LOCAL), np.float32)
    for u in range(16):
        v = base.index(here[u])
        for i in range(SHARD):
            out[u * SHARD + i, v * SHARD + i] = 1.0
    return out


def flip(a, mask):
    return lax.ppermute(a, "dp", [(i, i ^ mask) for i in range(32)])


def chip(a, mask):
    return flip(a, mask << 1)


def core(a):
    return flip(a, 1)


def rows(a):
    return lax.ppermute(a, "rows", [(0, 1), (1, 0)])


def along_z(a, pairs):
    return lax.ppermute(a, ("segment", "rows"), pairs)


def lanes(shape):
    return lax.broadcasted_iota(jnp.int32, shape, 1)


def rows_on(tiles, dr, low):
    if not dr:
        return tiles
    lane = lanes(tiles[0].shape)
    edge, step = (3, COLS) if dr > 0 else (0, 128 - COLS)
    here, there = (pltpu.roll(tiles[h * 4 + edge], step, 1) for h in (0, 1))
    inner = lane >= COLS if dr > 0 else lane < 128 - COLS
    upper = 1.0 - low
    to_here, to_there = (low, upper) if dr > 0 else (upper, low)
    ends = (jnp.where(inner, here, there * to_here), jnp.where(inner, there, here * to_there))
    out = []
    for h in (0, 1):
        part = tiles[h * 4 : h * 4 + 4]
        out += [ends[h], *part[:3]] if dr > 0 else [*part[1:], ends[h]]
    return out


def columns_on(tiles, dc):
    if not dc:
        return tiles
    col = lanes(tiles[0].shape) & (COLS - 1)
    valid = col >= 1 if dc > 0 else col <= COLS - 2
    return [jnp.where(valid, pltpu.roll(t, dc % 128, 1), 0.0) for t in tiles]


def added(one, other):
    return other if one is None else [a + b for a, b in zip(one, other)]


def tiles_of(ref, at, size):
    return [ref[pl.ds(at, size), t * 128 : (t + 1) * 128] for t in range(8)]


def columns_of(coef):
    return [jnp.broadcast_to(coef[:, i : i + 1], (coef.shape[0], 128)) for i in range(4)]


def assemble_body(fix_ref, *refs):
    parts, out_ref = refs[:-1], refs[-1]
    for p, (taps, order) in enumerate(GATHER_PARTS):
        own, far = parts[2 * p : 2 * p + 2]
        for t, k in enumerate(taps):
            at = slice(t * CH, (t + 1) * CH)
            if order:
                both = jnp.concatenate([own[:, at], far[:, at]], axis=0)
                out_ref[k * LOCAL : (k + 1) * LOCAL, :] = jnp.dot(
                    fix_ref[...], both, preferred_element_type=F32
                ).astype(BF16)
            else:
                out_ref[k * LOCAL : k * LOCAL + LOCAL // 2, :] = own[:, at]
                out_ref[k * LOCAL + LOCAL // 2 : (k + 1) * LOCAL, :] = far[:, at]


def call(body, args, outs, scratch, name, flops, in_bytes, aliases=None, scalars=()):
    return pl.pallas_call(
        body,
        in_specs=[pl.BlockSpec(memory_space=pltpu.SMEM)] * len(scalars)
        + [pl.BlockSpec(memory_space=pltpu.VMEM)] * len(args),
        out_specs=[pl.BlockSpec(memory_space=pltpu.VMEM)] * len(outs),
        out_shape=[jax.ShapeDtypeStruct(shape, dtype) for shape, dtype in outs],
        scratch_shapes=scratch,
        input_output_aliases=aliases or {},
        compiler_params=pltpu.CompilerParams(vmem_limit_bytes=VMEM),
        cost_estimate=pl.CostEstimate(flops=flops, bytes_accessed=in_bytes, transcendentals=0),
        name=name,
    )(*scalars, *args)


def back_body(low_ref, g0_ref, g1_ref, w_ref, a_ref, coef_ref, pre_ref, sums_ref, y_ref):
    low = low_ref[0].astype(F32)
    for k in range(9):
        for h, g_ref in enumerate((g0_ref, g1_ref)):
            y_ref[k * LOCAL : (k + 1) * LOCAL, h * HALF : (h + 1) * HALF] = jnp.dot(
                w_ref[k * LOCAL : (k + 1) * LOCAL, :], g_ref[...], preferred_element_type=F32
            )

    def strip(i, carry):
        at = pl.multiple_of(i * 8, 8)
        total = None
        for dc in (-1, 0, 1):
            part = None
            for dr in (-1, 0, 1):
                k = (dr + 1) * 3 + dc + 1
                part = added(part, rows_on(tiles_of(y_ref, k * LOCAL + at, 8), dr, low))
            total = added(total, columns_on(part, dc))
        mean, inv, gain, shift = columns_of(coef_ref[pl.ds(at, 8), :])
        s0, s1 = jnp.zeros((8, 128), F32), jnp.zeros((8, 128), F32)
        for t in range(8):
            a = a_ref[pl.ds(at, 8), t * 128 : (t + 1) * 128].astype(F32)
            normed = (a - mean) * inv
            preact = normed * gain + shift
            gate = jax.nn.sigmoid(preact)
            pre = total[t] * (gate * (1.0 + preact * (1.0 - gate)))
            pre_ref[pl.ds(at, 8), t * 128 : (t + 1) * 128] = pre
            s0, s1 = s0 + pre, s1 + pre * normed
        s0, s1 = jnp.sum(s0, axis=1, keepdims=True), jnp.sum(s1, axis=1, keepdims=True)
        lane = lanes((8, 128))
        sums_ref[pl.ds(at, 8), :] = jnp.where(lane == 0, s0, jnp.where(lane == 1, s1, 0.0))
        return carry

    lax.fori_loop(0, LOCAL // 8, strip, 0, unroll=4)


def back(low, g0, g1, w, a, coef):
    return call(
        back_body,
        (g0, g1, w, a, coef),
        [((LOCAL, PX), F32), ((LOCAL, 128), F32)],
        [pltpu.VMEM((9 * LOCAL, PX), F32)],
        "back",
        2 * 9 * LOCAL * CH * PX,
        5_000_000,
        scalars=(low,),
    )


def wgrad_body(accumulate, flags_ref, order_ref, unpick_ref, *refs):
    refs = list(refs)
    samples = [[refs.pop(0) for _ in range(8)] for _ in range(2)]
    count = 2 * len(SCATTER_PARTS)
    before = [refs.pop(0) for _ in range(count)] if accumulate else None
    outs = [refs.pop(0) for _ in range(count)]
    full = [[refs.pop(0) for _ in range(2)] for _ in range(2)]
    plain, ordered, shifted, adjoint = refs
    low = flags_ref[0].astype(F32)
    section = flags_ref[1]
    for o, (g0, g1, s00, s01, s10, s11, a_ref, coef_ref) in enumerate(samples):

        @pl.when(section == 1)
        def _():
            for h, g in enumerate((g0, g1)):
                full[o][h][...] = g[...]

        @pl.when(section == 0)
        def _():
            for h in (0, 1):
                total = None
                for b, (s, turned) in enumerate(((s00, 0), (s01, 1), (s10, 0), (s11, 1))):
                    at = (h ^ turned) * HALF
                    part = jnp.dot(
                        unpick_ref[b], s[:, at : at + HALF], preferred_element_type=F32
                    )
                    total = part if total is None else total + part
                full[o][h][...] = total.astype(BF16)

        for h in (0, 1):
            adjoint[:, o * PX + h * HALF : o * PX + (h + 1) * HALF] = full[o][h][...]

        def activate(i, carry):
            at = pl.multiple_of(i * 16, 16)
            mean, inv, gain, shift = columns_of(coef_ref[pl.ds(at, 16), :])
            for t in range(8):
                a = a_ref[pl.ds(at, 16), t * 128 : (t + 1) * 128].astype(F32)
                preact = (a - mean) * inv * gain + shift
                plain[pl.ds(at, 16), t * 128 : (t + 1) * 128] = (
                    preact * jax.nn.sigmoid(preact)
                ).astype(BF16)
            return carry

        lax.fori_loop(0, LOCAL // 16, activate, 0, unroll=5)
        for p, (taps, _) in enumerate(SCATTER_PARTS):
            ordered[...] = jnp.dot(order_ref[p], plain[...], preferred_element_type=F32)

            def build(i, carry):
                at = pl.multiple_of(i * 16, 16)
                tiles = tiles_of(ordered, at, 16)
                moved = {}
                for k in taps:
                    dr, dc = TAPS[k]
                    if dc not in moved:
                        moved[dc] = columns_on(tiles, -dc)
                    for t, y in enumerate(rows_on(moved[dc], -dr, low)):
                        at_px = o * PX + t * 128
                        shifted[pl.ds(k * LOCAL + at, 16), at_px : at_px + 128] = y.astype(BF16)
                return carry

            lax.fori_loop(0, LOCAL // 16, build, 0, unroll=5)
    for p, (taps, _) in enumerate(SCATTER_PARTS):
        for t, k in enumerate(taps):
            value = lax.dot_general(
                shifted[k * LOCAL : (k + 1) * LOCAL, :],
                adjoint[...],
                (((1,), (1,)), ((), ())),
                preferred_element_type=F32,
            )
            for side in (0, 1):
                part = value[side * LOCAL // 2 : (side + 1) * LOCAL // 2]
                at = slice(t * CH, (t + 1) * CH)
                if accumulate:
                    part = part + before[2 * p + side][:, at]
                outs[2 * p + side][:, at] = part


def wgrad(flags, unpick, samples, before=()):
    orders = jnp.asarray(np.stack([reorder(o) for _, o in SCATTER_PARTS]), BF16)
    outs = [((LOCAL // 2, len(taps) * CH), F32) for taps, _ in SCATTER_PARTS for _ in (0, 1)]
    args = [orders, unpick, *samples[0], *samples[1], *before]
    aliases = {1 + len(args) - len(before) + i: i for i in range(len(before))}
    got = call(
        lambda *refs: wgrad_body(bool(before), *refs),
        args,
        outs + [((CH, HALF), BF16)] * 4,
        [
            pltpu.VMEM((LOCAL, PX), BF16),
            pltpu.VMEM((LOCAL, PX), F32),
            pltpu.VMEM((9 * LOCAL, 2 * PX), BF16),
            pltpu.VMEM((CH, 2 * PX), BF16),
        ],
        "wgrad",
        2 * 2 * 9 * LOCAL * CH * PX,
        10_000_000,
        aliases,
        scalars=(flags,),
    )
    return got[: len(outs)], (got[-4:-2], got[-2:])


def spread(groups):
    return jnp.broadcast_to(groups[..., None], (*groups.shape, SHARD)).reshape(*groups.shape[:-1], LOCAL)


def slots(channels):
    return jnp.sum(channels.reshape(*channels.shape[:-1], 16, SHARD), axis=-1)


def over_four(x):
    x = x + core(x)
    return x + rows(x)


def turn_rows(a):
    return jnp.swapaxes(a.reshape(2, 4, 4, COLS, CH), 1, 2).reshape(2, HALF, CH)


def shards(segment_inputs, weights, gains, shifts, chain_cot, skip_cot):
    count_all = float(PX * CH // GROUPS)
    seg = lax.axis_index("segment")
    dp = lax.axis_index("dp")
    r = lax.axis_index("rows")
    c = dp % 2
    me = dp // 2
    low = jnp.stack([r, seg]).astype(jnp.int32)

    mine = lax.dynamic_slice_in_dim(weights[0], r * SHARD, SHARD, axis=1)
    gathered = [
        jnp.transpose(mine[taps[0] : taps[-1] + 1], (1, 0, 2)).reshape(SHARD, -1)
        for taps, _ in GATHER_PARTS
    ]
    for stage in (3, 2, 1):
        gathered = [
            jnp.concatenate([cur, chip(cur, ORDERS[order][stage])], axis=0)
            for cur, (_, order) in zip(gathered, GATHER_PARTS)
        ]
    weight_parts = []
    for cur, (_, order) in zip(gathered, GATHER_PARTS):
        weight_parts += [cur, chip(cur, ORDERS[order][0])]
    fix = jnp.asarray(reorder(GATHER_PARTS[1][1]).T, BF16)

    row = np.arange(CH)
    flips = np.asarray(slot_masks(ORDERS[0]))[row // SHARD % 16]
    natural = (
        40 * (me ^ jnp.asarray(flips, jnp.int32))
        + 20 * (c ^ jnp.asarray(row // 320, jnp.int32))
        + 10 * (r ^ jnp.asarray(row // LOCAL % 2, jnp.int32))
        + jnp.asarray(row % SHARD, jnp.int32)
    )
    hit = natural[:, None] == lax.broadcasted_iota(jnp.int32, (CH, CH), 1)
    pick = hit.astype(BF16)
    own_hit = hit[:LOCAL]
    eye = jnp.eye(CH, dtype=BF16)
    column = natural.reshape(4, 1, LOCAL)
    unpick = (column == lax.broadcasted_iota(jnp.int32, (4, CH, LOCAL), 1)).astype(BF16)

    total = chain_cot.astype(F32) + skip_cot.astype(F32)
    flat = turn_rows(total.astype(BF16))
    outer_t = jnp.einsum("ij,npj->nip", eye, flat, preferred_element_type=F32).astype(BF16)
    outer = []
    for n in range(2):
        near = outer_t[n]
        far = along_z(near, [(2, 3), (3, 2)] if n == 0 else [(1, 2), (0, 3)])
        outer.append(((near, far), (core(near), core(far))))

    local = turn_rows(segment_inputs[0])
    picked = jnp.einsum("ij,npj->nip", pick, local, preferred_element_type=F32).astype(BF16)
    picked = picked.reshape(2, 2, 2, LOCAL, HALF)
    both = jnp.concatenate([picked[:, :, 0], rows(picked[:, :, 1])], axis=-1)
    theirs = core(both[:, 1])
    inputs = [(both[n, 0], theirs[n]) for n in range(2)]

    sums = []
    for n in range(2):
        for o in range(2):
            wide = inputs[n][o].astype(F32)
            sums.append(jnp.stack([jnp.sum(wide, -1), jnp.sum(wide * wide, -1)]))
    local_sums = slots(jnp.stack(sums).reshape(2, 2, 2, LOCAL))
    local_sums = local_sums + core(local_sums)[:, ::-1]
    local_sums = local_sums + rows(local_sums)
    mean = local_sums[:, :, 0] / count_all
    inv = lax.rsqrt(local_sums[:, :, 1] / count_all - mean * mean + epsilon)
    gain = jnp.sum(jnp.where(own_hit, gains[0][None, :], 0.0), axis=1)
    shift = jnp.sum(jnp.where(own_hit, shifts[0][None, :], 0.0), axis=1)
    mean_c, inv_c = spread(mean), spread(inv)
    coef = jnp.stack(
        [mean_c, inv_c, jnp.broadcast_to(gain, mean_c.shape), jnp.broadcast_to(shift, mean_c.shape)],
        axis=-1,
    )
    coef = jnp.pad(coef, ((0, 0), (0, 0), (0, 0), (0, 124)))

    (w,) = call(
        assemble_body, (fix, *weight_parts), [((9 * LOCAL, CH), BF16)], [], "assemble", 10**8, 4_000_000
    )

    def in_grads(n, halves):
        pres, parts = [], []
        for o in range(2):
            pre, part = back(low, *halves[o], w, inputs[n][o], coef[n, o])
            pres.append(pre)
            parts.append(part[:, :2])
        s = jnp.stack(parts)
        group = slots(jnp.moveaxis(s * gain[None, :, None], 2, 1))
        group = group + core(group)[::-1]
        group = group + rows(group)
        grads = []
        for o in range(2):
            first = spread(group[o, 0] / count_all)[:, None]
            second = spread(group[o, 1] / count_all)[:, None]
            normed = (inputs[n][o].astype(F32) - mean_c[n, o][:, None]) * inv_c[n, o][:, None]
            grads.append(
                inv_c[n, o][:, None] * (pres[o] * gain[:, None] - first - normed * second)
            )
        return grads, s

    slices = []
    for n in range(2):
        grads, _ = in_grads(n, outer[n])
        got = []
        for o in range(2):
            one = along_z(grads[o].astype(BF16), [(2, 1), (3, 0)])
            got.append((along_z(one, [(0, 1), (1, 0)]), one))
        across = [tuple(core(a) for a in got[o]) for o in range(2)]
        slices.append([(*got[o], *across[1 - o]) for o in range(2)])

    weight_grads, adjoint = (), []
    for n in range(2):
        samples = [
            (*outer[n][o], *slices[n][o], inputs[n][o], coef[n, o]) for o in range(2)
        ]
        weight_grads, full = wgrad(low, unpick, samples, weight_grads)
        adjoint.append(full)

    scattered = []
    for p, (_, order) in enumerate(SCATTER_PARTS):
        keep, give = weight_grads[2 * p : 2 * p + 2]
        for stage in range(4):
            cur = keep + chip(give, ORDERS[order][stage])
            half = cur.shape[0] // 2
            keep, give = cur[:half], cur[half:]
        scattered.append(cur)
    taps = [k for part, _ in SCATTER_PARTS for k in part]
    shard = jnp.concatenate(scattered, axis=1).reshape(SHARD, 9, CH)
    shard = jnp.stack([shard[:, taps.index(k)] for k in range(9)])
    far_shard = rows(shard)
    weight_grad = jnp.where(
        r == 0,
        jnp.concatenate([shard, far_shard], axis=1),
        jnp.concatenate([far_shard, shard], axis=1),
    )

    results, norm_sums = [], 0.0
    for n in range(2):
        grads, s = in_grads(n, adjoint[n])
        norm_sums = norm_sums + jnp.sum(s, axis=0)
        split = []
        for o in range(2):
            high = lax.reduce_precision(grads[o], 8, 7)
            split.append(jnp.stack([high, grads[o] - high]).astype(BF16))
        two = jnp.stack([split[0], core(split[1])], axis=1)
        two = jnp.stack([two[..., :HALF], rows(two[..., HALF:])], axis=2).reshape(2, CH, HALF)
        nat = jnp.einsum("tjp,ji->tpi", two, pick, preferred_element_type=F32)
        nat = jnp.swapaxes(nat.reshape(2, 4, 4, COLS, CH), 1, 2).reshape(2, HALF // COLS, COLS, CH)
        wide = chain_cot[n].astype(F32) + skip_cot[n].astype(F32)
        results.append((nat[0] + jnp.where(seg == 0, nat[1] + wide, 0.0)).astype(BF16))
    outputs = jnp.stack(results)[None]

    spread_sums = jnp.sum(jnp.where(own_hit[:, None, :], norm_sums[:, :, None], 0.0), axis=0)
    for mask in (1, 2, 6, 8, 24):
        spread_sums = spread_sums + flip(spread_sums, mask)
    spread_sums = spread_sums + rows(spread_sums)
    return (outputs, weight_grad[None], spread_sums[1][None], spread_sums[0][None])


def solution(mesh):
    placed = (
        P("segment", "dp", "rows", None, None),
        P("segment", None, "dp", None),
        P("segment", None),
        P("segment", None),
        P("dp", "rows", None, None),
        P("dp", "rows", None, None),
    )
    return jax.shard_map(
        shards,
        mesh=mesh,
        in_specs=placed,
        out_specs=(
            P("segment", "dp", "rows", None, None),
            P("segment", None, "dp", None),
            P("segment", None),
            P("segment", None),
        ),
        check_vma=False,
    )
```

```python
import jax
import jax.numpy as jnp
import numpy as np
from jax import lax
from jax.experimental import pallas as pl
from jax.experimental.pallas import tpu as pltpu
from jax.sharding import PartitionSpec as P

GROUPS = 16
epsilon = 1e-05
F32 = jnp.float32
BF16 = jnp.bfloat16

CH = 640
PX = 1024
HALF = 512
COLS = 32
LOCAL = 160
SHARD = 10
TAPS = [(-1, -1), (-1, 0), (-1, 1), (0, -1), (0, 0), (0, 1), (1, -1), (1, 0), (1, 1)]

AX, BX, AY, BY = 1, 3, 4, 12
ORDERS = [(AX, BX, AY, BY), (BX, AX, BY, AY), (AY, BY, AX, BX), (BY, AY, BX, AX)]
GATHER_PARTS = [((0, 1, 2, 3, 4), 0), ((5, 6, 7, 8), 2)]
SCATTER_PARTS = [((0, 3), 0), ((1, 4), 1), ((2, 5), 2), ((6, 7, 8), 3)]

SEQUENCE = [k for part, _ in SCATTER_PARTS for k in part]

MIB = 1024 * 1024


def slot_masks(order):
    return [
        (u >> 3 & 1) * order[0] ^ (u >> 2 & 1) * order[1] ^ (u >> 1 & 1) * order[2] ^ (u & 1) * order[3]
        for u in range(16)
    ]


def reorder(order):
    here, base = slot_masks(ORDERS[order]), slot_masks(ORDERS[0])
    out = np.zeros((LOCAL, LOCAL), np.float32)
    for u in range(16):
        v = base.index(here[u])
        for i in range(SHARD):
            out[u * SHARD + i, v * SHARD + i] = 1.0
    return out


def flip(a, mask):
    return lax.ppermute(a, "dp", [(i, i ^ mask) for i in range(32)])


def chip(a, mask):
    return flip(a, mask << 1)


def core(a):
    return flip(a, 1)


def rows(a):
    return lax.ppermute(a, "rows", [(0, 1), (1, 0)])


def along_z(a, pairs):
    return lax.ppermute(a, ("segment", "rows"), pairs)


def lanes(shape):
    return lax.broadcasted_iota(jnp.int32, shape, 1)


def rows_on(tiles, dr, low):
    if not dr:
        return tiles
    lane = lanes(tiles[0].shape)
    edge, step = (3, COLS) if dr > 0 else (0, 128 - COLS)
    here, there = (pltpu.roll(tiles[h * 4 + edge], step, 1) for h in (0, 1))
    inner = lane >= COLS if dr > 0 else lane < 128 - COLS
    upper = 1.0 - low
    to_here, to_there = (low, upper) if dr > 0 else (upper, low)
    ends = (jnp.where(inner, here, there * to_here), jnp.where(inner, there, here * to_there))
    out = []
    for h in (0, 1):
        part = tiles[h * 4 : h * 4 + 4]
        out += [ends[h], *part[:3]] if dr > 0 else [*part[1:], ends[h]]
    return out


def columns_on(tiles, dc):
    if not dc:
        return tiles
    col = lanes(tiles[0].shape) & (COLS - 1)
    valid = col >= 1 if dc > 0 else col <= COLS - 2
    return [jnp.where(valid, pltpu.roll(t, dc % 128, 1), 0.0) for t in tiles]


def added(one, other):
    return other if one is None else [a + b for a, b in zip(one, other)]


def tiles_of(ref, at, size):
    return [ref[pl.ds(at, size), t * 128 : (t + 1) * 128] for t in range(8)]


def columns_of(coef):
    return [jnp.broadcast_to(coef[:, i : i + 1], (coef.shape[0], 128)) for i in range(4)]


def assemble_body(fix_ref, *refs):
    parts, out_ref = refs[:-1], refs[-1]
    for p, (taps, order) in enumerate(GATHER_PARTS):
        own, far = parts[2 * p : 2 * p + 2]
        for t, k in enumerate(taps):
            at = slice(t * CH, (t + 1) * CH)
            if order:
                both = jnp.concatenate([own[:, at], far[:, at]], axis=0)
                out_ref[k * LOCAL : (k + 1) * LOCAL, :] = jnp.dot(
                    fix_ref[...], both, preferred_element_type=F32
                ).astype(BF16)
            else:
                out_ref[k * LOCAL : k * LOCAL + LOCAL // 2, :] = own[:, at]
                out_ref[k * LOCAL + LOCAL // 2 : (k + 1) * LOCAL, :] = far[:, at]


def call(body, args, outs, scratch, name, flops, in_bytes, scalars=(), vmem=20):
    return pl.pallas_call(
        body,
        in_specs=[pl.BlockSpec(memory_space=pltpu.SMEM)] * len(scalars)
        + [pl.BlockSpec(memory_space=pltpu.VMEM)] * len(args),
        out_specs=[pl.BlockSpec(memory_space=pltpu.VMEM)] * len(outs),
        out_shape=[jax.ShapeDtypeStruct(shape, dtype) for shape, dtype in outs],
        scratch_shapes=scratch,
        compiler_params=pltpu.CompilerParams(vmem_limit_bytes=vmem * MIB),
        cost_estimate=pl.CostEstimate(flops=flops, bytes_accessed=in_bytes, transcendentals=0),
        name=name,
    )(*scalars, *args)


def back_body(low_ref, g0_ref, g1_ref, w_ref, a_ref, coef_ref, pre_ref, sums_ref, y_ref):
    low = low_ref[0].astype(F32)
    for k in range(9):
        for h, g_ref in enumerate((g0_ref, g1_ref)):
            y_ref[k * LOCAL : (k + 1) * LOCAL, h * HALF : (h + 1) * HALF] = jnp.dot(
                w_ref[k * LOCAL : (k + 1) * LOCAL, :], g_ref[...], preferred_element_type=F32
            )

    def strip(i, carry):
        at = pl.multiple_of(i * 8, 8)
        total = None
        for dc in (-1, 0, 1):
            part = None
            for dr in (-1, 0, 1):
                k = (dr + 1) * 3 + dc + 1
                part = added(part, rows_on(tiles_of(y_ref, k * LOCAL + at, 8), dr, low))
            total = added(total, columns_on(part, dc))
        mean, inv, gain, shift = columns_of(coef_ref[pl.ds(at, 8), :])
        s0, s1 = jnp.zeros((8, 128), F32), jnp.zeros((8, 128), F32)
        for t in range(8):
            a = a_ref[pl.ds(at, 8), t * 128 : (t + 1) * 128].astype(F32)
            normed = (a - mean) * inv
            preact = normed * gain + shift
            gate = jax.nn.sigmoid(preact)
            pre = total[t] * (gate * (1.0 + preact * (1.0 - gate)))
            pre_ref[pl.ds(at, 8), t * 128 : (t + 1) * 128] = pre
            s0, s1 = s0 + pre, s1 + pre * normed
        s0, s1 = jnp.sum(s0, axis=1, keepdims=True), jnp.sum(s1, axis=1, keepdims=True)
        lane = lanes((8, 128))
        sums_ref[pl.ds(at, 8), :] = jnp.where(lane == 0, s0, jnp.where(lane == 1, s1, 0.0))
        return carry

    lax.fori_loop(0, LOCAL // 8, strip, 0, unroll=4)


def back(low, g0, g1, w, a, coef):
    return call(
        back_body,
        (g0, g1, w, a, coef),
        [((LOCAL, PX), F32), ((LOCAL, 128), F32)],
        [pltpu.VMEM((9 * LOCAL, PX), F32)],
        "back",
        2 * 9 * LOCAL * CH * PX,
        5_000_000,
        scalars=(low,),
    )


def prepare_body(low_ref, order_ref, *refs):
    samples, (shifted, plain, ordered) = (refs[:2], refs[2:4]), refs[4:]
    low = low_ref[0].astype(F32)
    for o, (a_ref, coef_ref) in enumerate(samples):

        def activate(i, carry):
            at = pl.multiple_of(i * 16, 16)
            mean, inv, gain, shift = columns_of(coef_ref[pl.ds(at, 16), :])
            for t in range(8):
                a = a_ref[pl.ds(at, 16), t * 128 : (t + 1) * 128].astype(F32)
                preact = (a - mean) * inv * gain + shift
                plain[pl.ds(at, 16), t * 128 : (t + 1) * 128] = (
                    preact * jax.nn.sigmoid(preact)
                ).astype(BF16)
            return carry

        lax.fori_loop(0, LOCAL // 16, activate, 0, unroll=5)
        for p, (taps, _) in enumerate(SCATTER_PARTS):
            ordered[...] = jnp.dot(order_ref[p], plain[...], preferred_element_type=F32)

            def build(i, carry):
                at = pl.multiple_of(i * 16, 16)
                tiles = tiles_of(ordered, at, 16)
                moved = {}
                for k in taps:
                    dr, dc = TAPS[k]
                    if dc not in moved:
                        moved[dc] = columns_on(tiles, -dc)
                    for t, y in enumerate(rows_on(moved[dc], -dr, low)):
                        at_px = o * PX + t * 128
                        row = SEQUENCE.index(k) * LOCAL
                        shifted[pl.ds(row + at, 16), at_px : at_px + 128] = y.astype(BF16)
                return carry

            lax.fori_loop(0, LOCAL // 16, build, 0, unroll=5)


def prepare(low, samples):
    orders = jnp.asarray(np.stack([reorder(o) for _, o in SCATTER_PARTS]), BF16)
    return call(
        prepare_body,
        (orders, *samples[0], *samples[1]),
        [((9 * LOCAL, 2 * PX), BF16)],
        [pltpu.VMEM((LOCAL, PX), BF16), pltpu.VMEM((LOCAL, PX), F32)],
        "prepare",
        2 * 10**9,
        8_000_000,
        scalars=(low,),
    )[0]


def wgrad_body(accumulate, flags_ref, unpick_ref, *refs):
    refs = list(refs)
    samples = [[refs.pop(0) for _ in range(6)] for _ in range(2)]
    shifted = refs.pop(0)
    count = 2 * len(SCATTER_PARTS)
    before = [refs.pop(0) for _ in range(count)] if accumulate else None
    outs = [refs.pop(0) for _ in range(count)]
    full = [[refs.pop(0) for _ in range(2)] for _ in range(2)]
    (adjoint,) = refs
    section = flags_ref[1]
    step = pl.program_id(0)

    @pl.when(step == 0)
    def _():
        for o, (g0, g1, s00, s01, s10, s11) in enumerate(samples):

            @pl.when(section == 1)
            def _():
                for h, g in enumerate((g0, g1)):
                    full[o][h][...] = g[...]

            @pl.when(section == 0)
            def _():
                for h in (0, 1):
                    total = None
                    for b, (s, turned) in enumerate(((s00, 0), (s01, 1), (s10, 0), (s11, 1))):
                        at = (h ^ turned) * HALF
                        part = jnp.dot(
                            unpick_ref[b], s[:, at : at + HALF], preferred_element_type=F32
                        )
                        total = part if total is None else total + part
                    full[o][h][...] = total.astype(BF16)

            for h in (0, 1):
                at = o * PX + h * HALF
                adjoint[at : at + HALF, :] = full[o][h][...].T

    value = jnp.dot(shifted[...], adjoint[...], preferred_element_type=F32)
    for p, (taps, _) in enumerate(SCATTER_PARTS):
        start = SEQUENCE.index(taps[0])

        @pl.when((step >= start) & (step < start + len(taps)))
        def _():
            for side in (0, 1):
                part = value[side * LOCAL // 2 : (side + 1) * LOCAL // 2]
                if accumulate:
                    part = part + before[2 * p + side][0]
                outs[2 * p + side][0] = part


def wgrad(flags, unpick, samples, shifted, before=()):
    half = LOCAL // 2
    fixed = lambda a: pl.BlockSpec(a.shape, lambda g: (0,) * a.ndim, pipeline_mode=pl.Buffered(1))
    tap_specs, tap_shapes = [], []
    for taps, _ in SCATTER_PARTS:
        start, size = SEQUENCE.index(taps[0]), len(taps)
        for _ in (0, 1):
            tap_specs.append(
                pl.BlockSpec(
                    (1, half, CH),
                    lambda g, start=start, size=size: (jnp.clip(g - start, 0, size - 1), 0, 0),
                )
            )
            tap_shapes.append(jax.ShapeDtypeStruct((size, half, CH), F32))
    args = [unpick, *samples[0], *samples[1]]
    specs = [fixed(a) for a in args] + [pl.BlockSpec((LOCAL, 2 * PX), lambda g: (g, 0))]
    adjoint_spec = pl.BlockSpec((CH, HALF), lambda g: (0, 0))
    got = pl.pallas_call(
        lambda *refs: wgrad_body(bool(before), *refs),
        grid=(9,),
        in_specs=[pl.BlockSpec(memory_space=pltpu.SMEM)] + specs + (tap_specs if before else []),
        out_specs=tap_specs + [adjoint_spec] * 4,
        out_shape=tap_shapes + [jax.ShapeDtypeStruct((CH, HALF), BF16)] * 4,
        scratch_shapes=[pltpu.VMEM((2 * PX, CH), BF16)],
        input_output_aliases={2 + len(args) + i: i for i in range(len(before))},
        compiler_params=pltpu.CompilerParams(vmem_limit_bytes=32 * MIB),
        cost_estimate=pl.CostEstimate(
            flops=2 * 2 * 9 * LOCAL * CH * PX, bytes_accessed=16_000_000, transcendentals=0
        ),
        name="wgrad",
    )(flags, *args, shifted, *before)
    return got[:-4], (got[-4:-2], got[-2:])


def after(x, done):
    return lax.optimization_barrier((x, done))[0]


def spread(groups):
    return jnp.broadcast_to(groups[..., None], (*groups.shape, SHARD)).reshape(*groups.shape[:-1], LOCAL)


def slots(channels):
    return jnp.sum(channels.reshape(*channels.shape[:-1], 16, SHARD), axis=-1)


def over_four(x):
    x = x + core(x)
    return x + rows(x)


def turn_rows(a):
    return jnp.swapaxes(a.reshape(2, 4, 4, COLS, CH), 1, 2).reshape(2, HALF, CH)


def shards(segment_inputs, weights, gains, shifts, chain_cot, skip_cot):
    count_all = float(PX * CH // GROUPS)
    seg = lax.axis_index("segment")
    dp = lax.axis_index("dp")
    r = lax.axis_index("rows")
    c = dp % 2
    me = dp // 2
    low = jnp.stack([r, seg]).astype(jnp.int32)

    mine = lax.dynamic_slice_in_dim(weights[0], r * SHARD, SHARD, axis=1)
    gathered = [
        jnp.transpose(mine[taps[0] : taps[-1] + 1], (1, 0, 2)).reshape(SHARD, -1)
        for taps, _ in GATHER_PARTS
    ]
    for stage in (3, 2, 1):
        gathered = [
            jnp.concatenate([cur, chip(cur, ORDERS[order][stage])], axis=0)
            for cur, (_, order) in zip(gathered, GATHER_PARTS)
        ]
    weight_parts = []
    for cur, (_, order) in zip(gathered, GATHER_PARTS):
        weight_parts += [cur, chip(cur, ORDERS[order][0])]
    fix = jnp.asarray(reorder(GATHER_PARTS[1][1]).T, BF16)

    row = np.arange(CH)
    flips = np.asarray(slot_masks(ORDERS[0]))[row // SHARD % 16]
    natural = (
        40 * (me ^ jnp.asarray(flips, jnp.int32))
        + 20 * (c ^ jnp.asarray(row // 320, jnp.int32))
        + 10 * (r ^ jnp.asarray(row // LOCAL % 2, jnp.int32))
        + jnp.asarray(row % SHARD, jnp.int32)
    )
    hit = natural[:, None] == lax.broadcasted_iota(jnp.int32, (CH, CH), 1)
    pick = hit.astype(BF16)
    own_hit = hit[:LOCAL]
    eye = jnp.eye(CH, dtype=BF16)
    column = natural.reshape(4, 1, LOCAL)
    unpick = (column == lax.broadcasted_iota(jnp.int32, (4, CH, LOCAL), 1)).astype(BF16)

    total = chain_cot.astype(F32) + skip_cot.astype(F32)
    flat = turn_rows(total.astype(BF16))
    outer_t = jnp.einsum("ij,npj->nip", eye, flat, preferred_element_type=F32).astype(BF16)
    outer = []
    for n in range(2):
        near = outer_t[n]
        far = along_z(near, [(2, 3), (3, 2)] if n == 0 else [(1, 2), (0, 3)])
        outer.append(((near, far), (core(near), core(far))))

    local = turn_rows(segment_inputs[0])
    picked = jnp.einsum("ij,npj->nip", pick, local, preferred_element_type=F32).astype(BF16)
    wide = picked.astype(F32)
    stats = jnp.stack([jnp.sum(wide, -1), jnp.sum(wide * wide, -1)], axis=1)
    stats = jnp.sum(stats.reshape(2, 2, 4, 16, SHARD), axis=(2, 4))
    stats = stats + rows(stats)
    stats = jnp.stack([stats, core(stats)], axis=1)
    mean = stats[:, :, 0] / count_all
    inv = lax.rsqrt(stats[:, :, 1] / count_all - mean * mean + epsilon)
    picked = picked.reshape(2, 2, 2, LOCAL, HALF)
    both = jnp.concatenate([picked[:, :, 0], rows(picked[:, :, 1])], axis=-1)
    theirs = core(both[:, 1])
    inputs = [(both[n, 0], theirs[n]) for n in range(2)]

    gain = jnp.sum(jnp.where(own_hit, gains[0][None, :], 0.0), axis=1)
    shift = jnp.sum(jnp.where(own_hit, shifts[0][None, :], 0.0), axis=1)
    mean_c, inv_c = spread(mean), spread(inv)
    coef = jnp.stack(
        [mean_c, inv_c, jnp.broadcast_to(gain, mean_c.shape), jnp.broadcast_to(shift, mean_c.shape)],
        axis=-1,
    )
    coef = jnp.pad(coef, ((0, 0), (0, 0), (0, 0), (0, 124)))

    (w,) = call(
        assemble_body, (fix, *weight_parts), [((9 * LOCAL, CH), BF16)], [], "assemble", 10**8, 4_000_000
    )

    def in_grads(n, halves, earlier=None, gates=(None, None, None)):
        pres, parts = [], []
        for o in range(2):
            given = halves[o] if gates[o] is None else after(halves[o], gates[o])
            pre, part = back(low, *given, w, inputs[n][o], coef[n, o])
            pres.append(pre)
            parts.append(part[:, :2])
        s = jnp.stack(parts)
        group = slots(jnp.moveaxis(s * gain[None, :, None], 2, 1))
        turned = lambda g: jnp.concatenate([g[32:64], g[:32], g[64:]])
        packed = group.reshape(64)
        if earlier is not None:
            s = earlier + jnp.sum(s, axis=0)
            placed = jnp.sum(jnp.where(own_hit[:, None, :], s[:, :, None], 0.0), axis=0)
            packed = jnp.concatenate([packed, placed.reshape(2 * CH)])
        if gates[2] is not None:
            packed = after(packed, gates[2])
        packed = packed + turned(core(packed))
        packed = packed + rows(packed)
        group = packed[:64].reshape(2, 2, 16)
        grads = []
        for o in range(2):
            first = spread(group[o, 0] / count_all)[:, None]
            second = spread(group[o, 1] / count_all)[:, None]
            normed = (inputs[n][o].astype(F32) - mean_c[n, o][:, None]) * inv_c[n, o][:, None]
            grads.append(
                inv_c[n, o][:, None] * (pres[o] * gain[:, None] - first - normed * second)
            )
        return grads, (jnp.sum(s, axis=0) if earlier is None else packed[64:]), pres

    handed, hops = [], []
    for n in range(2):
        if n == 0:
            grads, _, _ = in_grads(n, outer[n])
        else:
            grads, _, _ = in_grads(n, outer[n], None, (handed[0], hops[0][0], hops[0][1]))
        handed.append([grads[o].astype(BF16) for o in range(2)])
        hops.append([along_z(handed[n][o], [(2, 1), (3, 0)]) for o in range(2)])
        if n == 0:
            shifted = [prepare(low, [(inputs[0][o], coef[0, o]) for o in range(2)])]
    last_coef = after(coef[1], handed[1])
    shifted.append(prepare(low, [(inputs[1][o], last_coef[o]) for o in range(2)]))
    slices = []
    for n in range(2):
        got = [(along_z(one, [(0, 1), (1, 0)]), one) for one in hops[n]]
        across = [tuple(core(a) for a in got[o]) for o in range(2)]
        slices.append([(*got[o], *across[1 - o]) for o in range(2)])

    def returned(n, grads):
        split = []
        for o in range(2):
            high = lax.reduce_precision(grads[o], 8, 7)
            split.append(jnp.stack([high, grads[o] - high]).astype(BF16))
        two = jnp.stack([split[0], core(split[1])], axis=1)
        arrived = rows(two[..., HALF:])
        two = jnp.stack([two[..., :HALF], arrived], axis=2).reshape(2, CH, HALF)
        nat = jnp.einsum("tjp,ji->tpi", two, pick, preferred_element_type=F32)
        nat = jnp.swapaxes(nat.reshape(2, 4, 4, COLS, CH), 1, 2).reshape(2, HALF // COLS, COLS, CH)
        wide = chain_cot[n].astype(F32) + skip_cot[n].astype(F32)
        return (nat[0] + jnp.where(seg == 0, nat[1] + wide, 0.0)).astype(BF16), arrived

    samples = [[(*outer[n][o], *slices[n][o]) for o in range(2)] for n in range(2)]
    weight_grads, full = wgrad(low, unpick, samples[0], shifted[0])
    weight_grads, last_full = wgrad(low, unpick, samples[1], shifted[1], weight_grads)

    sides = [weight_grads[2 * p : 2 * p + 2] for p in range(len(SCATTER_PARTS))]
    results = []
    for stage in range(4):
        came = [chip(give, ORDERS[order][stage]) for (_, give), (_, order) in zip(sides, SCATTER_PARTS)]
        came = lax.optimization_barrier(came)
        if stage == 0:
            grads, norm_sums, _ = in_grads(0, full, None, (weight_grads[0], None, None))
            value, arrived = returned(0, grads)
            results.append(value)
        if stage == 1:
            grads, norm_sums, _ = in_grads(1, last_full, norm_sums, (came[0], came[0], None))
            results.append(returned(1, grads)[0])
        if stage > 1:
            norm_sums = after(norm_sums, came[0])
            norm_sums = norm_sums + chip(norm_sums, ORDERS[0][stage - 2])
        now = [keep + c for (keep, _), c in zip(sides, came)]
        sides = [(a[:, : a.shape[1] // 2], a[:, a.shape[1] // 2 :]) for a in now]
    outputs = jnp.stack(results)[None]
    for mask in ORDERS[0][2:]:
        norm_sums = norm_sums + chip(norm_sums, mask)
    norm_sums = norm_sums.reshape(2, CH)
    shard = jnp.concatenate(now, axis=0)
    shard = jnp.stack([shard[SEQUENCE.index(k)] for k in range(9)])
    far_shard = rows(shard)
    weight_grad = jnp.where(
        r == 0,
        jnp.concatenate([shard, far_shard], axis=1),
        jnp.concatenate([far_shard, shard], axis=1),
    )
    return (outputs, weight_grad[None], norm_sums[1][None], norm_sums[0][None])


def solution(mesh):
    placed = (
        P("segment", "dp", "rows", None, None),
        P("segment", None, "dp", None),
        P("segment", None),
        P("segment", None),
        P("dp", "rows", None, None),
        P("dp", "rows", None, None),
    )
    return jax.shard_map(
        shards,
        mesh=mesh,
        in_specs=placed,
        out_specs=(
            P("segment", "dp", "rows", None, None),
            P("segment", None, "dp", None),
            P("segment", None),
            P("segment", None),
        ),
        check_vma=False,
    )
```

```python
import jax
import jax.numpy as jnp
import numpy as np
from jax import lax
from jax.experimental import pallas as pl
from jax.experimental.pallas import tpu as pltpu
from jax.sharding import PartitionSpec as P

GROUPS = 16
epsilon = 1e-05
F32 = jnp.float32
BF16 = jnp.bfloat16

CH = 640
PX = 1024
HALF = 512
COLS = 32
LOCAL = 160
SHARD = 10
TAPS = [(-1, -1), (-1, 0), (-1, 1), (0, -1), (0, 0), (0, 1), (1, -1), (1, 0), (1, 1)]

AX, BX, AY, BY = 1, 3, 4, 12
ORDERS = [(AX, BX, AY, BY), (BX, AX, BY, AY), (AY, BY, AX, BX), (BY, AY, BX, AX)]
GATHER_PARTS = [((0, 1, 2, 3, 4), 0), ((5, 6, 7, 8), 2)]
SCATTER_PARTS = [((0, 3, 6, 1, 4), 0), ((7, 2, 5, 8), 2)]

SEQUENCE = [k for part, _ in SCATTER_PARTS for k in part]

MIB = 1024 * 1024


def slot_masks(order):
    return [
        (u >> 3 & 1) * order[0] ^ (u >> 2 & 1) * order[1] ^ (u >> 1 & 1) * order[2] ^ (u & 1) * order[3]
        for u in range(16)
    ]


def reorder(order):
    here, base = slot_masks(ORDERS[order]), slot_masks(ORDERS[0])
    out = np.zeros((LOCAL, LOCAL), np.float32)
    for u in range(16):
        v = base.index(here[u])
        for i in range(SHARD):
            out[u * SHARD + i, v * SHARD + i] = 1.0
    return out


def flip(a, mask):
    return lax.ppermute(a, "dp", [(i, i ^ mask) for i in range(32)])


def chip(a, mask):
    return flip(a, mask << 1)


def core(a):
    return flip(a, 1)


def rows(a):
    return lax.ppermute(a, "rows", [(0, 1), (1, 0)])


def along_z(a, pairs):
    return lax.ppermute(a, ("segment", "rows"), pairs)


def lanes(shape):
    return lax.broadcasted_iota(jnp.int32, shape, 1)


def rows_on(tiles, dr, low):
    if not dr:
        return tiles
    lane = lanes(tiles[0].shape)
    edge, step = (3, COLS) if dr > 0 else (0, 128 - COLS)
    here, there = (pltpu.roll(tiles[h * 4 + edge], step, 1) for h in (0, 1))
    inner = lane >= COLS if dr > 0 else lane < 128 - COLS
    upper = 1.0 - low
    to_here, to_there = (low, upper) if dr > 0 else (upper, low)
    ends = (jnp.where(inner, here, there * to_here), jnp.where(inner, there, here * to_there))
    out = []
    for h in (0, 1):
        part = tiles[h * 4 : h * 4 + 4]
        out += [ends[h], *part[:3]] if dr > 0 else [*part[1:], ends[h]]
    return out


def columns_on(tiles, dc):
    if not dc:
        return tiles
    col = lanes(tiles[0].shape) & (COLS - 1)
    valid = col >= 1 if dc > 0 else col <= COLS - 2
    return [jnp.where(valid, pltpu.roll(t, dc % 128, 1), 0.0) for t in tiles]


def added(one, other):
    return other if one is None else [a + b for a, b in zip(one, other)]


def tiles_of(ref, at, size):
    return [ref[pl.ds(at, size), t * 128 : (t + 1) * 128] for t in range(8)]


def columns_of(coef):
    return [jnp.broadcast_to(coef[:, i : i + 1], (coef.shape[0], 128)) for i in range(4)]


def assemble_body(fix_ref, *refs):
    parts, out_ref = refs[:-1], refs[-1]
    for p, (taps, order) in enumerate(GATHER_PARTS):
        own, far = parts[2 * p : 2 * p + 2]
        for t, k in enumerate(taps):
            at = slice(t * CH, (t + 1) * CH)
            if order:
                both = jnp.concatenate([own[:, at], far[:, at]], axis=0)
                out_ref[k * LOCAL : (k + 1) * LOCAL, :] = jnp.dot(
                    fix_ref[...], both, preferred_element_type=F32
                ).astype(BF16)
            else:
                out_ref[k * LOCAL : k * LOCAL + LOCAL // 2, :] = own[:, at]
                out_ref[k * LOCAL + LOCAL // 2 : (k + 1) * LOCAL, :] = far[:, at]


def call(body, args, outs, scratch, name, flops, in_bytes, scalars=(), vmem=20):
    return pl.pallas_call(
        body,
        in_specs=[pl.BlockSpec(memory_space=pltpu.SMEM)] * len(scalars)
        + [pl.BlockSpec(memory_space=pltpu.VMEM)] * len(args),
        out_specs=[pl.BlockSpec(memory_space=pltpu.VMEM)] * len(outs),
        out_shape=[jax.ShapeDtypeStruct(shape, dtype) for shape, dtype in outs],
        scratch_shapes=scratch,
        compiler_params=pltpu.CompilerParams(vmem_limit_bytes=vmem * MIB),
        cost_estimate=pl.CostEstimate(flops=flops, bytes_accessed=in_bytes, transcendentals=0),
        name=name,
    )(*scalars, *args)


def back_body(low_ref, g0_ref, g1_ref, w_ref, a_ref, coef_ref, pre_ref, sums_ref, y_ref):
    low = low_ref[0].astype(F32)
    for k in range(9):
        for h, g_ref in enumerate((g0_ref, g1_ref)):
            y_ref[k * LOCAL : (k + 1) * LOCAL, h * HALF : (h + 1) * HALF] = jnp.dot(
                w_ref[k * LOCAL : (k + 1) * LOCAL, :], g_ref[...], preferred_element_type=F32
            )

    def strip(i, carry):
        at = pl.multiple_of(i * 8, 8)
        total = None
        for dc in (-1, 0, 1):
            part = None
            for dr in (-1, 0, 1):
                k = (dr + 1) * 3 + dc + 1
                part = added(part, rows_on(tiles_of(y_ref, k * LOCAL + at, 8), dr, low))
            total = added(total, columns_on(part, dc))
        mean, inv, gain, shift = columns_of(coef_ref[pl.ds(at, 8), :])
        s0, s1 = jnp.zeros((8, 128), F32), jnp.zeros((8, 128), F32)
        for t in range(8):
            a = a_ref[pl.ds(at, 8), t * 128 : (t + 1) * 128].astype(F32)
            normed = (a - mean) * inv
            preact = normed * gain + shift
            gate = jax.nn.sigmoid(preact)
            pre = total[t] * (gate * (1.0 + preact * (1.0 - gate)))
            pre_ref[pl.ds(at, 8), t * 128 : (t + 1) * 128] = pre
            s0, s1 = s0 + pre, s1 + pre * normed
        s0, s1 = jnp.sum(s0, axis=1, keepdims=True), jnp.sum(s1, axis=1, keepdims=True)
        lane = lanes((8, 128))
        sums_ref[pl.ds(at, 8), :] = jnp.where(lane == 0, s0, jnp.where(lane == 1, s1, 0.0))
        return carry

    lax.fori_loop(0, LOCAL // 8, strip, 0, unroll=4)


def back(low, g0, g1, w, a, coef):
    return call(
        back_body,
        (g0, g1, w, a, coef),
        [((LOCAL, PX), F32), ((LOCAL, 128), F32)],
        [pltpu.VMEM((9 * LOCAL, PX), F32)],
        "back",
        2 * 9 * LOCAL * CH * PX,
        5_000_000,
        scalars=(low,),
    )


def prepare_body(low_ref, order_ref, *refs):
    samples, (shifted, plain, ordered) = (refs[:2], refs[2:4]), refs[4:]
    low = low_ref[0].astype(F32)
    for o, (a_ref, coef_ref) in enumerate(samples):

        def activate(i, carry):
            at = pl.multiple_of(i * 16, 16)
            mean, inv, gain, shift = columns_of(coef_ref[pl.ds(at, 16), :])
            for t in range(8):
                a = a_ref[pl.ds(at, 16), t * 128 : (t + 1) * 128].astype(F32)
                preact = (a - mean) * inv * gain + shift
                plain[pl.ds(at, 16), t * 128 : (t + 1) * 128] = (
                    preact * jax.nn.sigmoid(preact)
                ).astype(BF16)
            return carry

        lax.fori_loop(0, LOCAL // 16, activate, 0, unroll=5)
        for p, (taps, _) in enumerate(SCATTER_PARTS):
            ordered[...] = jnp.dot(order_ref[p], plain[...], preferred_element_type=F32)

            def build(i, carry):
                at = pl.multiple_of(i * 16, 16)
                tiles = tiles_of(ordered, at, 16)
                moved = {}
                for k in taps:
                    dr, dc = TAPS[k]
                    if dc not in moved:
                        moved[dc] = columns_on(tiles, -dc)
                    for t, y in enumerate(rows_on(moved[dc], -dr, low)):
                        at_px = o * PX + t * 128
                        row = SEQUENCE.index(k) * LOCAL
                        shifted[pl.ds(row + at, 16), at_px : at_px + 128] = y.astype(BF16)
                return carry

            lax.fori_loop(0, LOCAL // 16, build, 0, unroll=5)


def prepare(low, samples):
    orders = jnp.asarray(np.stack([reorder(o) for _, o in SCATTER_PARTS]), BF16)
    return call(
        prepare_body,
        (orders, *samples[0], *samples[1]),
        [((9 * LOCAL, 2 * PX), BF16)],
        [pltpu.VMEM((LOCAL, PX), BF16), pltpu.VMEM((LOCAL, PX), F32)],
        "prepare",
        2 * 10**9,
        8_000_000,
        scalars=(low,),
    )[0]


def wgrad_body(accumulate, flags_ref, unpick_ref, *refs):
    refs = list(refs)
    samples = [[refs.pop(0) for _ in range(6)] for _ in range(2)]
    shifted = refs.pop(0)
    count = 2 * len(SCATTER_PARTS)
    before = [refs.pop(0) for _ in range(count)] if accumulate else None
    outs = [refs.pop(0) for _ in range(count)]
    full = [[refs.pop(0) for _ in range(2)] for _ in range(2)]
    (adjoint,) = refs
    section = flags_ref[1]
    step = pl.program_id(0)

    @pl.when(step == 0)
    def _():
        for o, (g0, g1, s00, s01, s10, s11) in enumerate(samples):

            @pl.when(section == 1)
            def _():
                for h, g in enumerate((g0, g1)):
                    full[o][h][...] = g[...]

            @pl.when(section == 0)
            def _():
                for h in (0, 1):
                    total = None
                    for b, (s, turned) in enumerate(((s00, 0), (s01, 1), (s10, 0), (s11, 1))):
                        at = (h ^ turned) * HALF
                        part = jnp.dot(
                            unpick_ref[b], s[:, at : at + HALF], preferred_element_type=F32
                        )
                        total = part if total is None else total + part
                    full[o][h][...] = total.astype(BF16)

            for h in (0, 1):
                at = o * PX + h * HALF
                adjoint[at : at + HALF, :] = full[o][h][...].T

    value = jnp.dot(shifted[...], adjoint[...], preferred_element_type=F32)
    for p, (taps, _) in enumerate(SCATTER_PARTS):
        start = SEQUENCE.index(taps[0])

        @pl.when((step >= start) & (step < start + len(taps)))
        def _():
            for side in (0, 1):
                part = value[side * LOCAL // 2 : (side + 1) * LOCAL // 2]
                if accumulate:
                    part = part + before[2 * p + side][0]
                outs[2 * p + side][0] = part


def wgrad(flags, unpick, samples, shifted, before=()):
    half = LOCAL // 2
    fixed = lambda a: pl.BlockSpec(a.shape, lambda g: (0,) * a.ndim, pipeline_mode=pl.Buffered(1))
    tap_specs, tap_shapes = [], []
    for taps, _ in SCATTER_PARTS:
        start, size = SEQUENCE.index(taps[0]), len(taps)
        for _ in (0, 1):
            tap_specs.append(
                pl.BlockSpec(
                    (1, half, CH),
                    lambda g, start=start, size=size: (jnp.clip(g - start, 0, size - 1), 0, 0),
                )
            )
            tap_shapes.append(jax.ShapeDtypeStruct((size, half, CH), F32))
    args = [unpick, *samples[0], *samples[1]]
    specs = [fixed(a) for a in args] + [pl.BlockSpec((LOCAL, 2 * PX), lambda g: (g, 0))]
    adjoint_spec = pl.BlockSpec((CH, HALF), lambda g: (0, 0))
    got = pl.pallas_call(
        lambda *refs: wgrad_body(bool(before), *refs),
        grid=(9,),
        in_specs=[pl.BlockSpec(memory_space=pltpu.SMEM)] + specs + (tap_specs if before else []),
        out_specs=tap_specs + [adjoint_spec] * 4,
        out_shape=tap_shapes + [jax.ShapeDtypeStruct((CH, HALF), BF16)] * 4,
        scratch_shapes=[pltpu.VMEM((2 * PX, CH), BF16)],
        input_output_aliases={2 + len(args) + i: i for i in range(len(before))},
        compiler_params=pltpu.CompilerParams(vmem_limit_bytes=32 * MIB),
        cost_estimate=pl.CostEstimate(
            flops=2 * 2 * 9 * LOCAL * CH * PX, bytes_accessed=16_000_000, transcendentals=0
        ),
        name="wgrad",
    )(flags, *args, shifted, *before)
    return got[:-4], (got[-4:-2], got[-2:])


def after(x, done):
    return lax.optimization_barrier((x, done))[0]


def merge_body(count, last, *refs):
    for p in range(count):
        total = refs[p][...] + refs[count + p][...]
        if last:
            refs[2 * count + p][...] = total
        else:
            half = total.shape[1] // 2
            refs[2 * count + 2 * p][...] = total[:, :half]
            refs[2 * count + 2 * p + 1][...] = total[:, half:]


def merge(keeps, came, last):
    outs = []
    for k in keeps:
        size, half = k.shape[0], k.shape[1] // 2
        outs += [((size, 2 * half, CH), F32)] if last else [((size, half, CH), F32)] * 2
    count = len(keeps)
    got = call(
        lambda *refs: merge_body(count, last, *refs), (*keeps, *came), outs, [], "merge", 10**6, 4 * 10**6
    )
    return got if last else [tuple(got[2 * p : 2 * p + 2]) for p in range(count)]


def spread(groups):
    return jnp.broadcast_to(groups[..., None], (*groups.shape, SHARD)).reshape(*groups.shape[:-1], LOCAL)


def slots(channels):
    return jnp.sum(channels.reshape(*channels.shape[:-1], 16, SHARD), axis=-1)


def over_four(x):
    x = x + core(x)
    return x + rows(x)


def turn_rows(a):
    return jnp.swapaxes(a.reshape(2, 4, 4, COLS, CH), 1, 2).reshape(2, HALF, CH)


def shards(segment_inputs, weights, gains, shifts, chain_cot, skip_cot):
    count_all = float(PX * CH // GROUPS)
    seg = lax.axis_index("segment")
    dp = lax.axis_index("dp")
    r = lax.axis_index("rows")
    c = dp % 2
    me = dp // 2
    low = jnp.stack([r, seg]).astype(jnp.int32)

    mine = lax.dynamic_slice_in_dim(weights[0], r * SHARD, SHARD, axis=1)
    gathered = [
        jnp.transpose(mine[taps[0] : taps[-1] + 1], (1, 0, 2)).reshape(SHARD, -1)
        for taps, _ in GATHER_PARTS
    ]
    for stage in (3, 2, 1):
        gathered = [
            jnp.concatenate([cur, chip(cur, ORDERS[order][stage])], axis=0)
            for cur, (_, order) in zip(gathered, GATHER_PARTS)
        ]
    weight_parts = []
    for cur, (_, order) in zip(gathered, GATHER_PARTS):
        weight_parts += [cur, chip(cur, ORDERS[order][0])]
    fix = jnp.asarray(reorder(GATHER_PARTS[1][1]).T, BF16)

    row = np.arange(CH)
    flips = np.asarray(slot_masks(ORDERS[0]))[row // SHARD % 16]
    natural = (
        40 * (me ^ jnp.asarray(flips, jnp.int32))
        + 20 * (c ^ jnp.asarray(row // 320, jnp.int32))
        + 10 * (r ^ jnp.asarray(row // LOCAL % 2, jnp.int32))
        + jnp.asarray(row % SHARD, jnp.int32)
    )
    hit = natural[:, None] == lax.broadcasted_iota(jnp.int32, (CH, CH), 1)
    pick = hit.astype(BF16)
    own_hit = hit[:LOCAL]
    eye = jnp.eye(CH, dtype=BF16)
    column = natural.reshape(4, 1, LOCAL)
    unpick = (column == lax.broadcasted_iota(jnp.int32, (4, CH, LOCAL), 1)).astype(BF16)

    total = chain_cot.astype(F32) + skip_cot.astype(F32)
    flat = turn_rows(total.astype(BF16))
    outer_t = jnp.einsum("ij,npj->nip", eye, flat, preferred_element_type=F32).astype(BF16)
    outer = []
    for n in range(2):
        near = outer_t[n]
        far = along_z(near, [(2, 3), (3, 2)] if n == 0 else [(1, 2), (0, 3)])
        outer.append(((near, far), (core(near), core(far))))

    local = turn_rows(segment_inputs[0])
    picked = jnp.einsum("ij,npj->nip", pick, local, preferred_element_type=F32).astype(BF16)
    wide = picked.astype(F32)
    stats = jnp.stack([jnp.sum(wide, -1), jnp.sum(wide * wide, -1)], axis=1)
    stats = jnp.sum(stats.reshape(2, 2, 4, 16, SHARD), axis=(2, 4))
    stats = stats + rows(stats)
    stats = jnp.stack([stats, core(stats)], axis=1)
    mean = stats[:, :, 0] / count_all
    inv = lax.rsqrt(stats[:, :, 1] / count_all - mean * mean + epsilon)
    picked = picked.reshape(2, 2, 2, LOCAL, HALF)
    both = jnp.concatenate([picked[:, :, 0], rows(picked[:, :, 1])], axis=-1)
    theirs = core(both[:, 1])
    inputs = [(both[n, 0], theirs[n]) for n in range(2)]

    gain = jnp.sum(jnp.where(own_hit, gains[0][None, :], 0.0), axis=1)
    shift = jnp.sum(jnp.where(own_hit, shifts[0][None, :], 0.0), axis=1)
    mean_c, inv_c = spread(mean), spread(inv)
    coef = jnp.stack(
        [mean_c, inv_c, jnp.broadcast_to(gain, mean_c.shape), jnp.broadcast_to(shift, mean_c.shape)],
        axis=-1,
    )
    coef = jnp.pad(coef, ((0, 0), (0, 0), (0, 0), (0, 124)))

    (w,) = call(
        assemble_body, (fix, *weight_parts), [((9 * LOCAL, CH), BF16)], [], "assemble", 10**8, 4_000_000
    )

    def in_grads(halves, gate=None, totals=False):
        pres, parts = [], []
        for n in range(2):
            for o in range(2):
                pre, part = back(low, *halves[n][o], w, inputs[n][o], coef[n, o])
                pres.append(pre)
                parts.append(part[:, :2])
        s = jnp.stack(parts)
        packed = slots(jnp.moveaxis(s * gain[None, :, None], 2, 1)).reshape(128)
        if totals:
            s = jnp.sum(s, axis=0)
            placed = jnp.sum(jnp.where(own_hit[:, None, :], s[:, :, None], 0.0), axis=0)
            packed = jnp.concatenate([packed, placed.reshape(2 * CH)])
        if gate is not None:
            packed = after(packed, gate)
        came = core(packed)
        came = [came[32:64], came[:32], came[96:128], came[64:96], came[128:]]
        packed = packed + jnp.concatenate(came)
        packed = packed + rows(packed)
        group = packed[:128].reshape(2, 2, 2, 16)
        grads = []
        for n in range(2):
            grads.append([])
            for o in range(2):
                first = spread(group[n, o, 0] / count_all)[:, None]
                second = spread(group[n, o, 1] / count_all)[:, None]
                normed = (inputs[n][o].astype(F32) - mean_c[n, o][:, None]) * inv_c[n, o][:, None]
                grads[n].append(
                    inv_c[n, o][:, None] * (pres[2 * n + o] * gain[:, None] - first - normed * second)
                )
        return grads, packed[128:]

    grads, _ = in_grads(outer)
    handed = [[grads[n][o].astype(BF16) for o in range(2)] for n in range(2)]
    shifted, slices, hops = [], [], None
    for n in range(2):
        ready = after(coef[n], handed[n])
        shifted.append(prepare(low, [(inputs[n][o], ready[o]) for o in range(2)]))
        pair = handed[n] if hops is None else after(handed[n], hops)
        hops = [along_z(a, [(2, 1), (3, 0)]) for a in pair]
        got = [(along_z(one, [(0, 1), (1, 0)]), one) for one in hops]
        across = [tuple(core(a) for a in got[o]) for o in range(2)]
        slices.append([(*got[o], *across[1 - o]) for o in range(2)])

    def returned(n, grads):
        split = []
        for o in range(2):
            high = lax.reduce_precision(grads[o], 8, 7)
            split.append(jnp.stack([high, grads[o] - high]).astype(BF16))
        two = jnp.stack([split[0], core(split[1])], axis=1)
        arrived = rows(two[..., HALF:])
        two = jnp.stack([two[..., :HALF], arrived], axis=2).reshape(2, CH, HALF)
        nat = jnp.einsum("tjp,ji->tpi", two, pick, preferred_element_type=F32)
        nat = jnp.swapaxes(nat.reshape(2, 4, 4, COLS, CH), 1, 2).reshape(2, HALF // COLS, COLS, CH)
        wide = chain_cot[n].astype(F32) + skip_cot[n].astype(F32)
        return (nat[0] + jnp.where(seg == 0, nat[1] + wide, 0.0)).astype(BF16), arrived

    samples = [[(*outer[n][o], *slices[n][o]) for o in range(2)] for n in range(2)]
    weight_grads, full = wgrad(low, unpick, samples[0], shifted[0])
    weight_grads, last_full = wgrad(low, unpick, samples[1], shifted[1], weight_grads)

    sides = [weight_grads[2 * p : 2 * p + 2] for p in range(len(SCATTER_PARTS))]
    for stage in range(4):
        came = [chip(give, ORDERS[order][stage]) for (_, give), (_, order) in zip(sides, SCATTER_PARTS)]
        came = lax.optimization_barrier(came)
        if stage == 0:
            grads, norm_sums = in_grads((full, last_full), came, True)
        if stage > 1:
            norm_sums = after(norm_sums, came)
            norm_sums = norm_sums + chip(norm_sums, ORDERS[0][stage - 2])
        sides = merge([keep for keep, _ in sides], came, stage == 3)
    now = sides
    results = [returned(n, grads[n])[0] for n in range(2)]
    outputs = jnp.stack(results)[None]
    for mask in ORDERS[0][2:]:
        norm_sums = norm_sums + chip(norm_sums, mask)
    norm_sums = norm_sums.reshape(2, CH)
    shard = jnp.concatenate(now, axis=0)
    shard = jnp.stack([shard[SEQUENCE.index(k)] for k in range(9)])
    far_shard = rows(shard)
    weight_grad = jnp.where(
        r == 0,
        jnp.concatenate([shard, far_shard], axis=1),
        jnp.concatenate([far_shard, shard], axis=1),
    )
    return (outputs, weight_grad[None], norm_sums[1][None], norm_sums[0][None])


def solution(mesh):
    placed = (
        P("segment", "dp", "rows", None, None),
        P("segment", None, "dp", None),
        P("segment", None),
        P("segment", None),
        P("dp", "rows", None, None),
        P("dp", "rows", None, None),
    )
    return jax.shard_map(
        shards,
        mesh=mesh,
        in_specs=placed,
        out_specs=(
            P("segment", "dp", "rows", None, None),
            P("segment", None, "dp", None),
            P("segment", None),
            P("segment", None),
        ),
        check_vma=False,
    )
```

```python
import jax
import jax.numpy as jnp
import numpy as np
from jax import lax
from jax.experimental import pallas as pl
from jax.experimental.pallas import tpu as pltpu
from jax.sharding import PartitionSpec as P

GROUPS = 16
epsilon = 1e-05
F32 = jnp.float32
BF16 = jnp.bfloat16

CH = 640
PX = 1024
HALF = 512
COLS = 32
LOCAL = 160
SHARD = 10
TAPS = [(-1, -1), (-1, 0), (-1, 1), (0, -1), (0, 0), (0, 1), (1, -1), (1, 0), (1, 1)]

AX, BX, AY, BY = 1, 3, 4, 12
ORDERS = [(AX, BX, AY, BY), (BX, AX, BY, AY), (AY, BY, AX, BX), (BY, AY, BX, AX)]
GATHER_PARTS = [((0, 1, 2, 3, 4), 0), ((5, 6, 7, 8), 2)]
SCATTER_PARTS = [((0, 3, 6, 1, 4), 0), ((7, 2, 5, 8), 2)]

SEQUENCE = [k for part, _ in SCATTER_PARTS for k in part]

MIB = 1024 * 1024


def slot_masks(order):
    return [
        (u >> 3 & 1) * order[0] ^ (u >> 2 & 1) * order[1] ^ (u >> 1 & 1) * order[2] ^ (u & 1) * order[3]
        for u in range(16)
    ]


def reorder(order):
    here, base = slot_masks(ORDERS[order]), slot_masks(ORDERS[0])
    out = np.zeros((LOCAL, LOCAL), np.float32)
    for u in range(16):
        v = base.index(here[u])
        for i in range(SHARD):
            out[u * SHARD + i, v * SHARD + i] = 1.0
    return out


def flip(a, mask):
    return lax.ppermute(a, "dp", [(i, i ^ mask) for i in range(32)])


def chip(a, mask):
    return flip(a, mask << 1)


def core(a):
    return flip(a, 1)


def rows(a):
    return lax.ppermute(a, "rows", [(0, 1), (1, 0)])


def along_z(a, pairs):
    return lax.ppermute(a, ("segment", "rows"), pairs)


def lanes(shape):
    return lax.broadcasted_iota(jnp.int32, shape, 1)


def rows_on(tiles, dr, low):
    if not dr:
        return tiles
    lane = lanes(tiles[0].shape)
    edge, step = (3, COLS) if dr > 0 else (0, 128 - COLS)
    here, there = (pltpu.roll(tiles[h * 4 + edge], step, 1) for h in (0, 1))
    inner = lane >= COLS if dr > 0 else lane < 128 - COLS
    upper = 1.0 - low
    to_here, to_there = (low, upper) if dr > 0 else (upper, low)
    ends = (jnp.where(inner, here, there * to_here), jnp.where(inner, there, here * to_there))
    out = []
    for h in (0, 1):
        part = tiles[h * 4 : h * 4 + 4]
        out += [ends[h], *part[:3]] if dr > 0 else [*part[1:], ends[h]]
    return out


def columns_on(tiles, dc):
    if not dc:
        return tiles
    col = lanes(tiles[0].shape) & (COLS - 1)
    valid = col >= 1 if dc > 0 else col <= COLS - 2
    return [jnp.where(valid, pltpu.roll(t, dc % 128, 1), 0.0) for t in tiles]


def added(one, other):
    return other if one is None else [a + b for a, b in zip(one, other)]


def tiles_of(ref, at, size):
    return [ref[pl.ds(at, size), t * 128 : (t + 1) * 128] for t in range(8)]


def columns_of(coef):
    return [jnp.broadcast_to(coef[:, i : i + 1], (coef.shape[0], 128)) for i in range(4)]


def assemble_body(fix_ref, *refs):
    parts, out_ref = refs[:-1], refs[-1]
    for p, (taps, order) in enumerate(GATHER_PARTS):
        own, far = parts[2 * p : 2 * p + 2]
        for t, k in enumerate(taps):
            at = slice(t * CH, (t + 1) * CH)
            if order:
                both = jnp.concatenate([own[:, at], far[:, at]], axis=0)
                out_ref[k * LOCAL : (k + 1) * LOCAL, :] = jnp.dot(
                    fix_ref[...], both, preferred_element_type=F32
                ).astype(BF16)
            else:
                out_ref[k * LOCAL : k * LOCAL + LOCAL // 2, :] = own[:, at]
                out_ref[k * LOCAL + LOCAL // 2 : (k + 1) * LOCAL, :] = far[:, at]


def call(body, args, outs, scratch, name, flops, in_bytes, scalars=(), vmem=20):
    return pl.pallas_call(
        body,
        in_specs=[pl.BlockSpec(memory_space=pltpu.SMEM)] * len(scalars)
        + [pl.BlockSpec(memory_space=pltpu.VMEM)] * len(args),
        out_specs=[pl.BlockSpec(memory_space=pltpu.VMEM)] * len(outs),
        out_shape=[jax.ShapeDtypeStruct(shape, dtype) for shape, dtype in outs],
        scratch_shapes=scratch,
        compiler_params=pltpu.CompilerParams(vmem_limit_bytes=vmem * MIB),
        cost_estimate=pl.CostEstimate(flops=flops, bytes_accessed=in_bytes, transcendentals=0),
        name=name,
    )(*scalars, *args)


def back_body(low_ref, g0_ref, g1_ref, w_ref, a_ref, coef_ref, pre_ref, sums_ref, y_ref):
    low = low_ref[0].astype(F32)
    for k in range(9):
        for h, g_ref in enumerate((g0_ref, g1_ref)):
            y_ref[k * LOCAL : (k + 1) * LOCAL, h * HALF : (h + 1) * HALF] = jnp.dot(
                w_ref[k * LOCAL : (k + 1) * LOCAL, :], g_ref[...], preferred_element_type=F32
            )

    def strip(i, carry):
        at = pl.multiple_of(i * 8, 8)
        total = None
        for dc in (-1, 0, 1):
            part = None
            for dr in (-1, 0, 1):
                k = (dr + 1) * 3 + dc + 1
                part = added(part, rows_on(tiles_of(y_ref, k * LOCAL + at, 8), dr, low))
            total = added(total, columns_on(part, dc))
        mean, inv, gain, shift = columns_of(coef_ref[pl.ds(at, 8), :])
        s0, s1 = jnp.zeros((8, 128), F32), jnp.zeros((8, 128), F32)
        for t in range(8):
            a = a_ref[pl.ds(at, 8), t * 128 : (t + 1) * 128].astype(F32)
            normed = (a - mean) * inv
            preact = normed * gain + shift
            gate = jax.nn.sigmoid(preact)
            pre = total[t] * (gate * (1.0 + preact * (1.0 - gate)))
            pre_ref[pl.ds(at, 8), t * 128 : (t + 1) * 128] = pre
            s0, s1 = s0 + pre, s1 + pre * normed
        s0, s1 = jnp.sum(s0, axis=1, keepdims=True), jnp.sum(s1, axis=1, keepdims=True)
        lane = lanes((8, 128))
        sums_ref[pl.ds(at, 8), :] = jnp.where(lane == 0, s0, jnp.where(lane == 1, s1, 0.0))
        return carry

    lax.fori_loop(0, LOCAL // 8, strip, 0, unroll=4)


def back(low, g0, g1, w, a, coef):
    return call(
        back_body,
        (g0, g1, w, a, coef),
        [((LOCAL, PX), F32), ((LOCAL, 128), F32)],
        [pltpu.VMEM((9 * LOCAL, PX), F32)],
        "back",
        2 * 9 * LOCAL * CH * PX,
        5_000_000,
        scalars=(low,),
    )


def prepare_body(low_ref, order_ref, *refs):
    samples, (shifted, plain, ordered) = (refs[:2], refs[2:4]), refs[4:]
    low = low_ref[0].astype(F32)
    for o, (a_ref, coef_ref) in enumerate(samples):

        def activate(i, carry):
            at = pl.multiple_of(i * 16, 16)
            mean, inv, gain, shift = columns_of(coef_ref[pl.ds(at, 16), :])
            for t in range(8):
                a = a_ref[pl.ds(at, 16), t * 128 : (t + 1) * 128].astype(F32)
                preact = (a - mean) * inv * gain + shift
                plain[pl.ds(at, 16), t * 128 : (t + 1) * 128] = (
                    preact * jax.nn.sigmoid(preact)
                ).astype(BF16)
            return carry

        lax.fori_loop(0, LOCAL // 16, activate, 0, unroll=5)
        for p, (taps, _) in enumerate(SCATTER_PARTS):
            ordered[...] = jnp.dot(order_ref[p], plain[...], preferred_element_type=F32)

            def build(i, carry):
                at = pl.multiple_of(i * 16, 16)
                tiles = tiles_of(ordered, at, 16)
                moved = {}
                for k in taps:
                    dr, dc = TAPS[k]
                    if dc not in moved:
                        moved[dc] = columns_on(tiles, -dc)
                    for t, y in enumerate(rows_on(moved[dc], -dr, low)):
                        at_px = o * PX + t * 128
                        row = SEQUENCE.index(k) * LOCAL
                        shifted[pl.ds(row + at, 16), at_px : at_px + 128] = y.astype(BF16)
                return carry

            lax.fori_loop(0, LOCAL // 16, build, 0, unroll=5)


def prepare(low, samples):
    orders = jnp.asarray(np.stack([reorder(o) for _, o in SCATTER_PARTS]), BF16)
    return call(
        prepare_body,
        (orders, *samples[0], *samples[1]),
        [((9 * LOCAL, 2 * PX), BF16)],
        [pltpu.VMEM((LOCAL, PX), BF16), pltpu.VMEM((LOCAL, PX), F32)],
        "prepare",
        2 * 10**9,
        8_000_000,
        scalars=(low,),
    )[0]


def wgrad_body(accumulate, flags_ref, unpick_ref, *refs):
    refs = list(refs)
    outer = [[refs.pop(0) for _ in range(2)] for _ in range(2)]
    slices = [refs.pop(0) for _ in range(4)]
    shifted = refs.pop(0)
    count = 2 * len(SCATTER_PARTS)
    before = [refs.pop(0) for _ in range(count)] if accumulate else None
    outs = [refs.pop(0) for _ in range(count)]
    full = [[refs.pop(0) for _ in range(2)] for _ in range(2)]
    (adjoint,) = refs
    section = flags_ref[1]
    step = pl.program_id(0)

    @pl.when(step == 0)
    def _():
        for o in (0, 1):

            @pl.when(section == 1)
            def _():
                for h in (0, 1):
                    full[o][h][...] = outer[o][h][...]

            @pl.when(section == 0)
            def _():
                for h in (0, 1):
                    total = None
                    for b in range(4):
                        at = (h ^ (b & 1)) * HALF
                        part = jnp.dot(
                            unpick_ref[b],
                            slices[b][o ^ (b >> 1), :, at : at + HALF],
                            preferred_element_type=F32,
                        )
                        total = part if total is None else total + part
                    full[o][h][...] = total.astype(BF16)

            for h in (0, 1):
                at = o * PX + h * HALF
                adjoint[at : at + HALF, :] = full[o][h][...].T

    value = jnp.dot(shifted[...], adjoint[...], preferred_element_type=F32)
    for p, (taps, _) in enumerate(SCATTER_PARTS):
        start = SEQUENCE.index(taps[0])

        @pl.when((step >= start) & (step < start + len(taps)))
        def _():
            for side in (0, 1):
                part = value[side * LOCAL // 2 : (side + 1) * LOCAL // 2]
                if accumulate:
                    part = part + before[2 * p + side][0]
                outs[2 * p + side][0] = part


def wgrad(flags, unpick, outer, slices, shifted, before=()):
    half = LOCAL // 2
    fixed = lambda a: pl.BlockSpec(a.shape, lambda g: (0,) * a.ndim, pipeline_mode=pl.Buffered(1))
    tap_specs, tap_shapes = [], []
    for taps, _ in SCATTER_PARTS:
        start, size = SEQUENCE.index(taps[0]), len(taps)
        for _ in (0, 1):
            tap_specs.append(
                pl.BlockSpec(
                    (1, half, CH),
                    lambda g, start=start, size=size: (jnp.clip(g - start, 0, size - 1), 0, 0),
                )
            )
            tap_shapes.append(jax.ShapeDtypeStruct((size, half, CH), F32))
    args = [unpick, *outer[0], *outer[1], *slices]
    specs = [fixed(a) for a in args] + [pl.BlockSpec((LOCAL, 2 * PX), lambda g: (g, 0))]
    adjoint_spec = pl.BlockSpec((CH, HALF), lambda g: (0, 0))
    got = pl.pallas_call(
        lambda *refs: wgrad_body(bool(before), *refs),
        grid=(9,),
        in_specs=[pl.BlockSpec(memory_space=pltpu.SMEM)] + specs + (tap_specs if before else []),
        out_specs=tap_specs + [adjoint_spec] * 4,
        out_shape=tap_shapes + [jax.ShapeDtypeStruct((CH, HALF), BF16)] * 4,
        scratch_shapes=[pltpu.VMEM((2 * PX, CH), BF16)],
        input_output_aliases={2 + len(args) + i: i for i in range(len(before))},
        compiler_params=pltpu.CompilerParams(vmem_limit_bytes=32 * MIB),
        cost_estimate=pl.CostEstimate(
            flops=2 * 2 * 9 * LOCAL * CH * PX, bytes_accessed=16_000_000, transcendentals=0
        ),
        name="wgrad",
    )(flags, *args, shifted, *before)
    return got[:-4], (got[-4:-2], got[-2:])


def after(x, done):
    return lax.optimization_barrier((x, done))[0]


def merge_body(count, last, *refs):
    for p in range(count):
        total = refs[p][...] + refs[count + p][...]
        if last:
            refs[2 * count + p][...] = total
        else:
            half = total.shape[1] // 2
            refs[2 * count + 2 * p][...] = total[:, :half]
            refs[2 * count + 2 * p + 1][...] = total[:, half:]


def merge(keeps, came, last):
    outs = []
    for k in keeps:
        size, half = k.shape[0], k.shape[1] // 2
        outs += [((size, 2 * half, CH), F32)] if last else [((size, half, CH), F32)] * 2
    count = len(keeps)
    got = call(
        lambda *refs: merge_body(count, last, *refs), (*keeps, *came), outs, [], "merge", 10**6, 4 * 10**6
    )
    return got if last else [tuple(got[2 * p : 2 * p + 2]) for p in range(count)]


def spread(groups):
    return jnp.broadcast_to(groups[..., None], (*groups.shape, SHARD)).reshape(*groups.shape[:-1], LOCAL)


def slots(channels):
    return jnp.sum(channels.reshape(*channels.shape[:-1], 16, SHARD), axis=-1)


def over_four(x):
    x = x + core(x)
    return x + rows(x)


def turn_rows(a):
    return jnp.swapaxes(a.reshape(2, 4, 4, COLS, CH), 1, 2).reshape(2, HALF, CH)


def shards(segment_inputs, weights, gains, shifts, chain_cot, skip_cot):
    count_all = float(PX * CH // GROUPS)
    seg = lax.axis_index("segment")
    dp = lax.axis_index("dp")
    r = lax.axis_index("rows")
    c = dp % 2
    me = dp // 2
    low = jnp.stack([r, seg]).astype(jnp.int32)

    mine = lax.dynamic_slice_in_dim(weights[0], r * SHARD, SHARD, axis=1)
    gathered = [
        jnp.transpose(mine[taps[0] : taps[-1] + 1], (1, 0, 2)).reshape(SHARD, -1)
        for taps, _ in GATHER_PARTS
    ]
    first = None
    for stage in (3, 2, 1):
        came = [chip(cur, ORDERS[order][stage]) for cur, (_, order) in zip(gathered, GATHER_PARTS)]
        gathered = [jnp.concatenate([cur, other], axis=0) for cur, other in zip(gathered, came)]
        if first is None:
            first = gathered
    weight_parts = []
    for cur, (_, order) in zip(gathered, GATHER_PARTS):
        weight_parts += [cur, chip(cur, ORDERS[order][0])]
    fix = jnp.asarray(reorder(GATHER_PARTS[1][1]).T, BF16)

    row = np.arange(CH)
    flips = np.asarray(slot_masks(ORDERS[0]))[row // SHARD % 16]
    natural = (
        40 * (me ^ jnp.asarray(flips, jnp.int32))
        + 20 * (c ^ jnp.asarray(row // 320, jnp.int32))
        + 10 * (r ^ jnp.asarray(row // LOCAL % 2, jnp.int32))
        + jnp.asarray(row % SHARD, jnp.int32)
    )
    hit = natural[:, None] == lax.broadcasted_iota(jnp.int32, (CH, CH), 1)
    pick = hit.astype(BF16)
    own_hit = hit[:LOCAL]
    eye = jnp.eye(CH, dtype=BF16)
    column = natural.reshape(4, 1, LOCAL)
    unpick = (column == lax.broadcasted_iota(jnp.int32, (4, CH, LOCAL), 1)).astype(BF16)

    total = chain_cot.astype(F32) + skip_cot.astype(F32)
    flat = turn_rows(total.astype(BF16))
    outer_t = jnp.einsum("ij,npj->nip", eye, flat, preferred_element_type=F32).astype(BF16)
    outer = []
    for n in range(2):
        near = outer_t[n]
        far = along_z(near, [(2, 3), (3, 2)] if n == 0 else [(1, 2), (0, 3)])
        outer.append(((near, far), (core(near), core(far))))

    local = turn_rows(after(segment_inputs[0], first))
    picked = jnp.einsum("ij,npj->nip", pick, local, preferred_element_type=F32).astype(BF16)
    wide = picked.astype(F32)
    stats = jnp.stack([jnp.sum(wide, -1), jnp.sum(wide * wide, -1)], axis=1)
    stats = jnp.sum(stats.reshape(2, 2, 4, 16, SHARD), axis=(2, 4))
    stats = stats + rows(stats)
    stats = jnp.stack([stats, core(stats)], axis=1)
    mean = stats[:, :, 0] / count_all
    inv = lax.rsqrt(stats[:, :, 1] / count_all - mean * mean + epsilon)
    picked = picked.reshape(2, 2, 2, LOCAL, HALF)
    both = jnp.concatenate([picked[:, :, 0], rows(picked[:, :, 1])], axis=-1)
    theirs = core(both[:, 1])
    inputs = [(both[n, 0], theirs[n]) for n in range(2)]

    gain = jnp.sum(jnp.where(own_hit, gains[0][None, :], 0.0), axis=1)
    shift = jnp.sum(jnp.where(own_hit, shifts[0][None, :], 0.0), axis=1)
    mean_c, inv_c = spread(mean), spread(inv)
    coef = jnp.stack(
        [mean_c, inv_c, jnp.broadcast_to(gain, mean_c.shape), jnp.broadcast_to(shift, mean_c.shape)],
        axis=-1,
    )
    coef = jnp.pad(coef, ((0, 0), (0, 0), (0, 0), (0, 124)))

    (w,) = call(
        assemble_body, (fix, *weight_parts), [((9 * LOCAL, CH), BF16)], [], "assemble", 10**8, 4_000_000
    )

    def in_grads(halves, gate=None, totals=False):
        pres, parts = [], []
        for n in range(2):
            for o in range(2):
                pre, part = back(low, *halves[n][o], w, inputs[n][o], coef[n, o])
                pres.append(pre)
                parts.append(part[:, :2])
        s = jnp.stack(parts)
        packed = slots(jnp.moveaxis(s * gain[None, :, None], 2, 1)).reshape(128)
        if totals:
            s = jnp.sum(s, axis=0)
            placed = jnp.sum(jnp.where(own_hit[:, None, :], s[:, :, None], 0.0), axis=0)
            packed = jnp.concatenate([packed, placed.reshape(2 * CH)])
        if gate is not None:
            packed = after(packed, gate)
        came = core(packed)
        came = [came[32:64], came[:32], came[96:128], came[64:96], came[128:]]
        packed = packed + jnp.concatenate(came)
        packed = packed + rows(packed)
        group = packed[:128].reshape(2, 2, 2, 16)
        grads = []
        for n in range(2):
            grads.append([])
            for o in range(2):
                first = spread(group[n, o, 0] / count_all)[:, None]
                second = spread(group[n, o, 1] / count_all)[:, None]
                normed = (inputs[n][o].astype(F32) - mean_c[n, o][:, None]) * inv_c[n, o][:, None]
                grads[n].append(
                    inv_c[n, o][:, None] * (pres[2 * n + o] * gain[:, None] - first - normed * second)
                )
        return grads, packed[128:]

    grads, _ = in_grads(outer)
    handed = [jnp.stack(grads[n]).astype(BF16) for n in range(2)]
    ready = after(coef, handed)
    shifted = [prepare(low, [(inputs[n][o], ready[n, o]) for o in range(2)]) for n in range(2)]
    slices, hops = [], None
    for n in range(2):
        pair = handed[n] if hops is None else after(handed[n], hops)
        hops = along_z(pair, [(2, 1), (3, 0)])
        if n == 0:
            hops = after(hops, shifted)
        two = along_z(hops, [(0, 1), (1, 0)])
        slices.append((two, hops, core(two), core(hops)))

    def returned(n, grads):
        split = []
        for o in range(2):
            high = lax.reduce_precision(grads[o], 8, 7)
            split.append(jnp.stack([high, grads[o] - high]).astype(BF16))
        two = jnp.stack([split[0], core(split[1])], axis=1)
        arrived = rows(two[..., HALF:])
        two = jnp.stack([two[..., :HALF], arrived], axis=2).reshape(2, CH, HALF)
        nat = jnp.einsum("tjp,ji->tpi", two, pick, preferred_element_type=F32)
        nat = jnp.swapaxes(nat.reshape(2, 4, 4, COLS, CH), 1, 2).reshape(2, HALF // COLS, COLS, CH)
        wide = chain_cot[n].astype(F32) + skip_cot[n].astype(F32)
        return (nat[0] + jnp.where(seg == 0, nat[1] + wide, 0.0)).astype(BF16), arrived

    weight_grads, full = wgrad(low, unpick, outer[0], slices[0], shifted[0])
    weight_grads, last_full = wgrad(low, unpick, outer[1], slices[1], shifted[1], weight_grads)
    full = after(full, weight_grads)

    sides = [weight_grads[2 * p : 2 * p + 2] for p in range(len(SCATTER_PARTS))]
    for stage in range(4):
        came = [chip(give, ORDERS[order][stage]) for (_, give), (_, order) in zip(sides, SCATTER_PARTS)]
        came = lax.optimization_barrier(came)
        if stage == 0:
            grads, norm_sums = in_grads((full, last_full), came, True)
        if stage > 1:
            norm_sums = after(norm_sums, came)
            norm_sums = norm_sums + chip(norm_sums, ORDERS[0][stage - 2])
        sides = merge([keep for keep, _ in sides], came, stage == 3)
    now = sides
    results = [returned(n, grads[n])[0] for n in range(2)]
    outputs = jnp.stack(results)[None]
    for mask in ORDERS[0][2:]:
        norm_sums = norm_sums + chip(norm_sums, mask)
    norm_sums = norm_sums.reshape(2, CH)
    shard = jnp.concatenate(now, axis=0)
    shard = jnp.stack([shard[SEQUENCE.index(k)] for k in range(9)])
    far_shard = rows(shard)
    weight_grad = jnp.where(
        r == 0,
        jnp.concatenate([shard, far_shard], axis=1),
        jnp.concatenate([far_shard, shard], axis=1),
    )
    return (outputs, weight_grad[None], norm_sums[1][None], norm_sums[0][None])


def solution(mesh):
    placed = (
        P("segment", "dp", "rows", None, None),
        P("segment", None, "dp", None),
        P("segment", None),
        P("segment", None),
        P("dp", "rows", None, None),
        P("dp", "rows", None, None),
    )
    return jax.shard_map(
        shards,
        mesh=mesh,
        in_specs=placed,
        out_specs=(
            P("segment", "dp", "rows", None, None),
            P("segment", None, "dp", None),
            P("segment", None),
            P("segment", None),
        ),
        check_vma=False,
    )
```

```python
import jax
import jax.numpy as jnp
import numpy as np
from jax import lax
from jax.experimental import pallas as pl
from jax.experimental.pallas import tpu as pltpu
from jax.sharding import PartitionSpec as P

GROUPS = 16
epsilon = 1e-05
F32 = jnp.float32
BF16 = jnp.bfloat16

CH = 640
PX = 1024
HALF = 512
COLS = 32
LOCAL = 160
SHARD = 10
TAPS = [(-1, -1), (-1, 0), (-1, 1), (0, -1), (0, 0), (0, 1), (1, -1), (1, 0), (1, 1)]

AX, BX, AY, BY = 1, 3, 4, 12
ORDERS = [(AX, BX, AY, BY), (BX, AX, BY, AY), (AY, BY, AX, BX), (BY, AY, BX, AX)]
GATHER_PARTS = [((0, 1, 2, 3, 4), 0), ((5, 6, 7, 8), 2)]
SCATTER_PARTS = [((0, 3, 6, 1, 4), 0), ((7, 2, 5, 8), 2)]

SEQUENCE = [k for part, _ in SCATTER_PARTS for k in part]

MIB = 1024 * 1024


def slot_masks(order):
    return [
        (u >> 3 & 1) * order[0] ^ (u >> 2 & 1) * order[1] ^ (u >> 1 & 1) * order[2] ^ (u & 1) * order[3]
        for u in range(16)
    ]


def reorder(order):
    here, base = slot_masks(ORDERS[order]), slot_masks(ORDERS[0])
    out = np.zeros((LOCAL, LOCAL), np.float32)
    for u in range(16):
        v = base.index(here[u])
        for i in range(SHARD):
            out[u * SHARD + i, v * SHARD + i] = 1.0
    return out


def flip(a, mask):
    return lax.ppermute(a, "dp", [(i, i ^ mask) for i in range(32)])


def chip(a, mask):
    return flip(a, mask << 1)


def core(a):
    return flip(a, 1)


def rows(a):
    return lax.ppermute(a, "rows", [(0, 1), (1, 0)])


def along_z(a, pairs):
    return lax.ppermute(a, ("segment", "rows"), pairs)


def lanes(shape):
    return lax.broadcasted_iota(jnp.int32, shape, 1)


def rows_on(tiles, dr, low):
    if not dr:
        return tiles
    lane = lanes(tiles[0].shape)
    edge, step = (3, COLS) if dr > 0 else (0, 128 - COLS)
    here, there = (pltpu.roll(tiles[h * 4 + edge], step, 1) for h in (0, 1))
    inner = lane >= COLS if dr > 0 else lane < 128 - COLS
    upper = 1.0 - low
    to_here, to_there = (low, upper) if dr > 0 else (upper, low)
    ends = (jnp.where(inner, here, there * to_here), jnp.where(inner, there, here * to_there))
    out = []
    for h in (0, 1):
        part = tiles[h * 4 : h * 4 + 4]
        out += [ends[h], *part[:3]] if dr > 0 else [*part[1:], ends[h]]
    return out


def columns_on(tiles, dc):
    if not dc:
        return tiles
    col = lanes(tiles[0].shape) & (COLS - 1)
    valid = col >= 1 if dc > 0 else col <= COLS - 2
    return [jnp.where(valid, pltpu.roll(t, dc % 128, 1), 0.0) for t in tiles]


def added(one, other):
    return other if one is None else [a + b for a, b in zip(one, other)]


def tiles_of(ref, at, size):
    return [ref[pl.ds(at, size), t * 128 : (t + 1) * 128] for t in range(8)]


def columns_of(coef):
    return [jnp.broadcast_to(coef[:, i : i + 1], (coef.shape[0], 128)) for i in range(4)]


def assemble_body(fix_ref, *refs):
    parts, out_ref = refs[:-1], refs[-1]
    for p, (taps, order) in enumerate(GATHER_PARTS):
        own, far = parts[2 * p : 2 * p + 2]
        for t, k in enumerate(taps):
            at = slice(t * CH, (t + 1) * CH)
            if order:
                both = jnp.concatenate([own[:, at], far[:, at]], axis=0)
                out_ref[k * LOCAL : (k + 1) * LOCAL, :] = jnp.dot(
                    fix_ref[...], both, preferred_element_type=F32
                ).astype(BF16)
            else:
                out_ref[k * LOCAL : k * LOCAL + LOCAL // 2, :] = own[:, at]
                out_ref[k * LOCAL + LOCAL // 2 : (k + 1) * LOCAL, :] = far[:, at]


def call(body, args, outs, scratch, name, flops, in_bytes, scalars=(), vmem=20):
    return pl.pallas_call(
        body,
        in_specs=[pl.BlockSpec(memory_space=pltpu.SMEM)] * len(scalars)
        + [pl.BlockSpec(memory_space=pltpu.VMEM)] * len(args),
        out_specs=[pl.BlockSpec(memory_space=pltpu.VMEM)] * len(outs),
        out_shape=[jax.ShapeDtypeStruct(shape, dtype) for shape, dtype in outs],
        scratch_shapes=scratch,
        compiler_params=pltpu.CompilerParams(vmem_limit_bytes=vmem * MIB),
        cost_estimate=pl.CostEstimate(flops=flops, bytes_accessed=in_bytes, transcendentals=0),
        name=name,
    )(*scalars, *args)


def back_body(low_ref, g0_ref, g1_ref, w_ref, a_ref, coef_ref, pre_ref, sums_ref, y_ref):
    low = low_ref[0].astype(F32)
    for k in range(9):
        for h, g_ref in enumerate((g0_ref, g1_ref)):
            y_ref[k * LOCAL : (k + 1) * LOCAL, h * HALF : (h + 1) * HALF] = jnp.dot(
                w_ref[k * LOCAL : (k + 1) * LOCAL, :], g_ref[...], preferred_element_type=F32
            )

    def strip(i, carry):
        at = pl.multiple_of(i * 8, 8)
        total = None
        for dc in (-1, 0, 1):
            part = None
            for dr in (-1, 0, 1):
                k = (dr + 1) * 3 + dc + 1
                part = added(part, rows_on(tiles_of(y_ref, k * LOCAL + at, 8), dr, low))
            total = added(total, columns_on(part, dc))
        mean, inv, gain, shift = columns_of(coef_ref[pl.ds(at, 8), :])
        s0, s1 = jnp.zeros((8, 128), F32), jnp.zeros((8, 128), F32)
        for t in range(8):
            a = a_ref[pl.ds(at, 8), t * 128 : (t + 1) * 128].astype(F32)
            normed = (a - mean) * inv
            preact = normed * gain + shift
            gate = jax.nn.sigmoid(preact)
            pre = total[t] * (gate * (1.0 + preact * (1.0 - gate)))
            pre_ref[pl.ds(at, 8), t * 128 : (t + 1) * 128] = pre
            s0, s1 = s0 + pre, s1 + pre * normed
        s0, s1 = jnp.sum(s0, axis=1, keepdims=True), jnp.sum(s1, axis=1, keepdims=True)
        lane = lanes((8, 128))
        sums_ref[pl.ds(at, 8), :] = jnp.where(lane == 0, s0, jnp.where(lane == 1, s1, 0.0))
        return carry

    lax.fori_loop(0, LOCAL // 8, strip, 0, unroll=4)


def back(low, g0, g1, w, a, coef):
    return call(
        back_body,
        (g0, g1, w, a, coef),
        [((LOCAL, PX), F32), ((LOCAL, 128), F32)],
        [pltpu.VMEM((9 * LOCAL, PX), F32)],
        "back",
        2 * 9 * LOCAL * CH * PX,
        5_000_000,
        scalars=(low,),
    )


def prepare_body(low_ref, order_ref, *refs):
    samples, (shifted, plain, ordered) = (refs[:2], refs[2:4]), refs[4:]
    low = low_ref[0].astype(F32)
    for o, (a_ref, coef_ref) in enumerate(samples):

        def activate(i, carry):
            at = pl.multiple_of(i * 16, 16)
            mean, inv, gain, shift = columns_of(coef_ref[pl.ds(at, 16), :])
            for t in range(8):
                a = a_ref[pl.ds(at, 16), t * 128 : (t + 1) * 128].astype(F32)
                preact = (a - mean) * inv * gain + shift
                plain[pl.ds(at, 16), t * 128 : (t + 1) * 128] = (
                    preact * jax.nn.sigmoid(preact)
                ).astype(BF16)
            return carry

        lax.fori_loop(0, LOCAL // 16, activate, 0, unroll=5)
        for p, (taps, _) in enumerate(SCATTER_PARTS):
            ordered[...] = jnp.dot(order_ref[p], plain[...], preferred_element_type=F32)

            def build(i, carry):
                at = pl.multiple_of(i * 16, 16)
                tiles = tiles_of(ordered, at, 16)
                moved = {}
                for k in taps:
                    dr, dc = TAPS[k]
                    if dc not in moved:
                        moved[dc] = columns_on(tiles, -dc)
                    for t, y in enumerate(rows_on(moved[dc], -dr, low)):
                        at_px = o * PX + t * 128
                        row = SEQUENCE.index(k) * LOCAL
                        shifted[pl.ds(row + at, 16), at_px : at_px + 128] = y.astype(BF16)
                return carry

            lax.fori_loop(0, LOCAL // 16, build, 0, unroll=5)


def prepare(low, samples):
    orders = jnp.asarray(np.stack([reorder(o) for _, o in SCATTER_PARTS]), BF16)
    return call(
        prepare_body,
        (orders, *samples[0], *samples[1]),
        [((9 * LOCAL, 2 * PX), BF16)],
        [pltpu.VMEM((LOCAL, PX), BF16), pltpu.VMEM((LOCAL, PX), F32)],
        "prepare",
        2 * 10**9,
        8_000_000,
        scalars=(low,),
    )[0]


def wgrad_body(accumulate, flags_ref, unpick_ref, *refs):
    refs = list(refs)
    outer = [[refs.pop(0) for _ in range(2)] for _ in range(2)]
    slices = [refs.pop(0) for _ in range(4)]
    shifted = refs.pop(0)
    count = 2 * len(SCATTER_PARTS)
    before = [refs.pop(0) for _ in range(count)] if accumulate else None
    outs = [refs.pop(0) for _ in range(count)]
    full = [[refs.pop(0) for _ in range(2)] for _ in range(2)]
    (adjoint,) = refs
    section = flags_ref[1]
    step = pl.program_id(0)

    @pl.when(step == 0)
    def _():
        for o in (0, 1):

            @pl.when(section == 1)
            def _():
                for h in (0, 1):
                    full[o][h][...] = outer[o][h][...]

            @pl.when(section == 0)
            def _():
                for h in (0, 1):
                    total = None
                    for b in range(4):
                        at = (h ^ (b & 1)) * HALF
                        part = jnp.dot(
                            unpick_ref[b],
                            slices[b][o ^ (b >> 1), :, at : at + HALF],
                            preferred_element_type=F32,
                        )
                        total = part if total is None else total + part
                    full[o][h][...] = total.astype(BF16)

            for h in (0, 1):
                at = o * PX + h * HALF
                adjoint[at : at + HALF, :] = full[o][h][...].T

    value = jnp.dot(shifted[...], adjoint[...], preferred_element_type=F32)
    for p, (taps, _) in enumerate(SCATTER_PARTS):
        start = SEQUENCE.index(taps[0])

        @pl.when((step >= start) & (step < start + len(taps)))
        def _():
            for side in (0, 1):
                part = value[side * LOCAL // 2 : (side + 1) * LOCAL // 2]
                if accumulate:
                    part = part + before[2 * p + side][0]
                outs[2 * p + side][0] = part


def wgrad(flags, unpick, outer, slices, shifted, before=()):
    half = LOCAL // 2
    fixed = lambda a: pl.BlockSpec(a.shape, lambda g: (0,) * a.ndim, pipeline_mode=pl.Buffered(1))
    tap_specs, tap_shapes = [], []
    for taps, _ in SCATTER_PARTS:
        start, size = SEQUENCE.index(taps[0]), len(taps)
        for _ in (0, 1):
            tap_specs.append(
                pl.BlockSpec(
                    (1, half, CH),
                    lambda g, start=start, size=size: (jnp.clip(g - start, 0, size - 1), 0, 0),
                )
            )
            tap_shapes.append(jax.ShapeDtypeStruct((size, half, CH), F32))
    args = [unpick, *outer[0], *outer[1], *slices]
    specs = [fixed(a) for a in args] + [pl.BlockSpec((LOCAL, 2 * PX), lambda g: (g, 0))]
    adjoint_spec = pl.BlockSpec((CH, HALF), lambda g: (0, 0))
    got = pl.pallas_call(
        lambda *refs: wgrad_body(bool(before), *refs),
        grid=(9,),
        in_specs=[pl.BlockSpec(memory_space=pltpu.SMEM)] + specs + (tap_specs if before else []),
        out_specs=tap_specs + [adjoint_spec] * 4,
        out_shape=tap_shapes + [jax.ShapeDtypeStruct((CH, HALF), BF16)] * 4,
        scratch_shapes=[pltpu.VMEM((2 * PX, CH), BF16)],
        input_output_aliases={2 + len(args) + i: i for i in range(len(before))},
        compiler_params=pltpu.CompilerParams(vmem_limit_bytes=32 * MIB),
        cost_estimate=pl.CostEstimate(
            flops=2 * 2 * 9 * LOCAL * CH * PX, bytes_accessed=16_000_000, transcendentals=0
        ),
        name="wgrad",
    )(flags, *args, shifted, *before)
    return got[:-4], (got[-4:-2], got[-2:])


def after(x, done):
    return lax.optimization_barrier((x, done))[0]


def merge_body(count, last, *refs):
    for p in range(count):
        total = refs[p][...] + refs[count + p][...]
        if last:
            refs[2 * count + p][...] = total
        else:
            half = total.shape[1] // 2
            refs[2 * count + 2 * p][...] = total[:, :half]
            refs[2 * count + 2 * p + 1][...] = total[:, half:]


def merge(keeps, came, last):
    outs = []
    for k in keeps:
        size, half = k.shape[0], k.shape[1] // 2
        outs += [((size, 2 * half, CH), F32)] if last else [((size, half, CH), F32)] * 2
    count = len(keeps)
    got = call(
        lambda *refs: merge_body(count, last, *refs), (*keeps, *came), outs, [], "merge", 10**6, 4 * 10**6
    )
    return got if last else [tuple(got[2 * p : 2 * p + 2]) for p in range(count)]


def spread(groups):
    return jnp.broadcast_to(groups[..., None], (*groups.shape, SHARD)).reshape(*groups.shape[:-1], LOCAL)


def slots(channels):
    return jnp.sum(channels.reshape(*channels.shape[:-1], 16, SHARD), axis=-1)


def over_four(x):
    x = x + core(x)
    return x + rows(x)


def turn_rows(a):
    return jnp.swapaxes(a.reshape(2, 4, 4, COLS, CH), 1, 2).reshape(2, HALF, CH)


def shards(segment_inputs, weights, gains, shifts, chain_cot, skip_cot):
    count_all = float(PX * CH // GROUPS)
    seg = lax.axis_index("segment")
    dp = lax.axis_index("dp")
    r = lax.axis_index("rows")
    c = dp % 2
    me = dp // 2
    low = jnp.stack([r, seg]).astype(jnp.int32)

    mine = lax.dynamic_slice_in_dim(weights[0], r * SHARD, SHARD, axis=1)
    gathered = [
        jnp.transpose(mine[taps[0] : taps[-1] + 1], (1, 0, 2)).reshape(SHARD, -1)
        for taps, _ in GATHER_PARTS
    ]
    for stage in (3, 2, 1):
        came = [chip(cur, ORDERS[order][stage]) for cur, (_, order) in zip(gathered, GATHER_PARTS)]
        gathered = [jnp.concatenate([cur, other], axis=0) for cur, other in zip(gathered, came)]
        if stage == 2:
            early = gathered
    weight_parts = []
    for cur, (_, order) in zip(gathered, GATHER_PARTS):
        weight_parts += [cur, chip(cur, ORDERS[order][0])]
    fix = jnp.asarray(reorder(GATHER_PARTS[1][1]).T, BF16)

    row = np.arange(CH)
    flips = np.asarray(slot_masks(ORDERS[0]))[row // SHARD % 16]
    natural = (
        40 * (me ^ jnp.asarray(flips, jnp.int32))
        + 20 * (c ^ jnp.asarray(row // 320, jnp.int32))
        + 10 * (r ^ jnp.asarray(row // LOCAL % 2, jnp.int32))
        + jnp.asarray(row % SHARD, jnp.int32)
    )
    hit = natural[:, None] == lax.broadcasted_iota(jnp.int32, (CH, CH), 1)
    pick = hit.astype(BF16)
    own_hit = hit[:LOCAL]
    eye = jnp.eye(CH, dtype=BF16)
    column = natural.reshape(4, 1, LOCAL)
    unpick = (column == lax.broadcasted_iota(jnp.int32, (4, CH, LOCAL), 1)).astype(BF16)

    total = chain_cot.astype(F32) + skip_cot.astype(F32)
    flat = turn_rows(total.astype(BF16))
    outer_t = jnp.einsum("ij,npj->nip", eye, flat, preferred_element_type=F32).astype(BF16)
    outer = []
    for n in range(2):
        near = outer_t[n]
        far = along_z(near, [(2, 3), (3, 2)] if n == 0 else [(1, 2), (0, 3)])
        outer.append(((near, far), (core(near), core(far))))

    local = turn_rows(after(segment_inputs[0], early))
    picked = jnp.einsum("ij,npj->nip", pick, local, preferred_element_type=F32).astype(BF16)
    wide = picked.astype(F32)
    stats = jnp.stack([jnp.sum(wide, -1), jnp.sum(wide * wide, -1)], axis=1)
    stats = jnp.sum(stats.reshape(2, 2, 4, 16, SHARD), axis=(2, 4))
    stats = stats + rows(stats)
    stats = jnp.stack([stats, core(stats)], axis=1)
    mean = stats[:, :, 0] / count_all
    inv = lax.rsqrt(stats[:, :, 1] / count_all - mean * mean + epsilon)
    picked = picked.reshape(2, 2, 2, LOCAL, HALF)
    both = jnp.concatenate([picked[:, :, 0], rows(picked[:, :, 1])], axis=-1)
    theirs = core(both[:, 1])
    inputs = [(both[n, 0], theirs[n]) for n in range(2)]

    gain = jnp.sum(jnp.where(own_hit, gains[0][None, :], 0.0), axis=1)
    shift = jnp.sum(jnp.where(own_hit, shifts[0][None, :], 0.0), axis=1)
    mean_c, inv_c = spread(mean), spread(inv)
    coef = jnp.stack(
        [mean_c, inv_c, jnp.broadcast_to(gain, mean_c.shape), jnp.broadcast_to(shift, mean_c.shape)],
        axis=-1,
    )
    coef = jnp.pad(coef, ((0, 0), (0, 0), (0, 0), (0, 124)))

    (w,) = call(
        assemble_body, (fix, *weight_parts), [((9 * LOCAL, CH), BF16)], [], "assemble", 10**8, 4_000_000
    )

    def in_grads(halves, gate=None, totals=False):
        pres, parts = [], []
        for n in range(2):
            for o in range(2):
                pre, part = back(low, *halves[n][o], w, inputs[n][o], coef[n, o])
                pres.append(pre)
                parts.append(part[:, :2])
        s = jnp.stack(parts)
        packed = slots(jnp.moveaxis(s * gain[None, :, None], 2, 1)).reshape(128)
        if totals:
            s = jnp.sum(s, axis=0)
            placed = jnp.sum(jnp.where(own_hit[:, None, :], s[:, :, None], 0.0), axis=0)
            packed = jnp.concatenate([packed, placed.reshape(2 * CH)])
        if gate is not None:
            packed = after(packed, gate)
        came = core(packed)
        came = [came[32:64], came[:32], came[96:128], came[64:96], came[128:]]
        packed = packed + jnp.concatenate(came)
        packed = packed + rows(packed)
        group = packed[:128].reshape(2, 2, 2, 16)
        grads = []
        for n in range(2):
            grads.append([])
            for o in range(2):
                first = spread(group[n, o, 0] / count_all)[:, None]
                second = spread(group[n, o, 1] / count_all)[:, None]
                normed = (inputs[n][o].astype(F32) - mean_c[n, o][:, None]) * inv_c[n, o][:, None]
                grads[n].append(
                    inv_c[n, o][:, None] * (pres[2 * n + o] * gain[:, None] - first - normed * second)
                )
        return grads, packed[128:]

    grads, _ = in_grads(outer)
    handed = [jnp.stack(grads[n]).astype(BF16) for n in range(2)]
    ready = after(coef, handed)
    shifted = [prepare(low, [(inputs[n][o], ready[n, o]) for o in range(2)]) for n in range(2)]
    slices, hops = [], None
    for n in range(2):
        pair = handed[n] if hops is None else after(handed[n], hops)
        hops = along_z(pair, [(2, 1), (3, 0)])
        if n == 0:
            hops = after(hops, shifted)
        two = along_z(hops, [(0, 1), (1, 0)])
        slices.append((two, hops, core(hops)))

    def to_owner(grads):
        split = []
        for n in range(2):
            for o in range(2):
                high = lax.reduce_precision(grads[n][o], 8, 7)
                split.append(jnp.stack([high, grads[n][o] - high]).astype(BF16))
        other = core(jnp.stack(split[1::2]))
        return jnp.stack([jnp.stack(split[0::2]), other], axis=2), other

    def returned(two):
        two = jnp.stack([two[..., :HALF], rows(two[..., HALF:])], axis=3).reshape(2, 2, CH, HALF)
        nat = jnp.einsum("ntjp,ji->ntpi", two, pick, preferred_element_type=F32)
        nat = jnp.swapaxes(nat.reshape(2, 2, 4, 4, COLS, CH), 2, 3)
        nat = nat.reshape(2, 2, HALF // COLS, COLS, CH)
        wide = chain_cot.astype(F32) + skip_cot.astype(F32)
        return (nat[:, 0] + jnp.where(seg == 0, nat[:, 1] + wide, 0.0)).astype(BF16)

    two, one, across = slices[0]
    weight_grads, full = wgrad(low, unpick, outer[0], (two, one, core(two), across), shifted[0])
    two, one, across = slices[1]
    two = after(two, weight_grads)
    weight_grads, last_full = wgrad(
        low, unpick, outer[1], (two, one, core(two), across), shifted[1], weight_grads
    )
    full = after(full, weight_grads)

    sides = [weight_grads[2 * p : 2 * p + 2] for p in range(len(SCATTER_PARTS))]
    for stage in range(4):
        came = [chip(give, ORDERS[order][stage]) for (_, give), (_, order) in zip(sides, SCATTER_PARTS)]
        came = lax.optimization_barrier(came)
        if stage == 0:
            grads, norm_sums = in_grads((full, last_full), came, True)
            homeward, other = to_owner(grads)
        if stage == 1:
            came = after(came, other)
        if stage > 1:
            norm_sums = after(norm_sums, came)
            norm_sums = norm_sums + chip(norm_sums, ORDERS[0][stage - 2])
        sides = merge([keep for keep, _ in sides], came, stage == 3)
    now = sides
    outputs = returned(homeward)[None]
    for mask in ORDERS[0][2:]:
        norm_sums = norm_sums + chip(norm_sums, mask)
    norm_sums = norm_sums.reshape(2, CH)
    shard = jnp.concatenate(now, axis=0)
    shard = jnp.stack([shard[SEQUENCE.index(k)] for k in range(9)])
    far_shard = rows(shard)
    weight_grad = jnp.where(
        r == 0,
        jnp.concatenate([shard, far_shard], axis=1),
        jnp.concatenate([far_shard, shard], axis=1),
    )
    return (outputs, weight_grad[None], norm_sums[1][None], norm_sums[0][None])


def solution(mesh):
    placed = (
        P("segment", "dp", "rows", None, None),
        P("segment", None, "dp", None),
        P("segment", None),
        P("segment", None),
        P("dp", "rows", None, None),
        P("dp", "rows", None, None),
    )
    return jax.shard_map(
        shards,
        mesh=mesh,
        in_specs=placed,
        out_specs=(
            P("segment", "dp", "rows", None, None),
            P("segment", None, "dp", None),
            P("segment", None),
            P("segment", None),
        ),
        check_vma=False,
    )
```

```python
import jax
import jax.numpy as jnp
import numpy as np
from jax import lax
from jax.experimental import pallas as pl
from jax.experimental.pallas import tpu as pltpu
from jax.sharding import PartitionSpec as P

GROUPS = 16
epsilon = 1e-05
F32 = jnp.float32
BF16 = jnp.bfloat16

CH = 640
PX = 1024
HALF = 512
COLS = 32
LOCAL = 160
SHARD = 10
TAPS = [(-1, -1), (-1, 0), (-1, 1), (0, -1), (0, 0), (0, 1), (1, -1), (1, 0), (1, 1)]

AX, BX, AY, BY = 1, 3, 4, 12
ORDERS = [(AX, BX, AY, BY), (BX, AX, BY, AY), (AY, BY, AX, BX), (BY, AY, BX, AX)]
GATHER_PARTS = [((0, 1, 2, 3, 4), 0), ((5, 6, 7, 8), 2)]
SCATTER_PARTS = [((0, 3, 6, 1, 4), 0), ((7, 2, 5, 8), 2)]

SEQUENCE = [k for part, _ in SCATTER_PARTS for k in part]

MIB = 1024 * 1024


def slot_masks(order):
    return [
        (u >> 3 & 1) * order[0] ^ (u >> 2 & 1) * order[1] ^ (u >> 1 & 1) * order[2] ^ (u & 1) * order[3]
        for u in range(16)
    ]


def reorder(order):
    here, base = slot_masks(ORDERS[order]), slot_masks(ORDERS[0])
    out = np.zeros((LOCAL, LOCAL), np.float32)
    for u in range(16):
        v = base.index(here[u])
        for i in range(SHARD):
            out[u * SHARD + i, v * SHARD + i] = 1.0
    return out


def flip(a, mask):
    return lax.ppermute(a, "dp", [(i, i ^ mask) for i in range(32)])


def chip(a, mask):
    return flip(a, mask << 1)


def core(a):
    return flip(a, 1)


def rows(a):
    return lax.ppermute(a, "rows", [(0, 1), (1, 0)])


def along_z(a, pairs):
    return lax.ppermute(a, ("segment", "rows"), pairs)


def lanes(shape):
    return lax.broadcasted_iota(jnp.int32, shape, 1)


def rows_on(tiles, dr, low):
    if not dr:
        return tiles
    lane = lanes(tiles[0].shape)
    edge, step = (3, COLS) if dr > 0 else (0, 128 - COLS)
    here, there = (pltpu.roll(tiles[h * 4 + edge], step, 1) for h in (0, 1))
    inner = lane >= COLS if dr > 0 else lane < 128 - COLS
    upper = 1.0 - low
    to_here, to_there = (low, upper) if dr > 0 else (upper, low)
    ends = (jnp.where(inner, here, there * to_here), jnp.where(inner, there, here * to_there))
    out = []
    for h in (0, 1):
        part = tiles[h * 4 : h * 4 + 4]
        out += [ends[h], *part[:3]] if dr > 0 else [*part[1:], ends[h]]
    return out


def columns_on(tiles, dc):
    if not dc:
        return tiles
    col = lanes(tiles[0].shape) & (COLS - 1)
    valid = col >= 1 if dc > 0 else col <= COLS - 2
    return [jnp.where(valid, pltpu.roll(t, dc % 128, 1), 0.0) for t in tiles]


def added(one, other):
    return other if one is None else [a + b for a, b in zip(one, other)]


def tiles_of(ref, at, size):
    return [ref[pl.ds(at, size), t * 128 : (t + 1) * 128] for t in range(8)]


def columns_of(coef):
    return [jnp.broadcast_to(coef[:, i : i + 1], (coef.shape[0], 128)) for i in range(4)]


def assemble_body(fix_ref, *refs):
    parts, out_ref = refs[:-1], refs[-1]
    for p, (taps, order) in enumerate(GATHER_PARTS):
        own, far = parts[2 * p : 2 * p + 2]
        for t, k in enumerate(taps):
            at = slice(t * CH, (t + 1) * CH)
            if order:
                both = jnp.concatenate([own[:, at], far[:, at]], axis=0)
                out_ref[k * LOCAL : (k + 1) * LOCAL, :] = jnp.dot(
                    fix_ref[...], both, preferred_element_type=F32
                ).astype(BF16)
            else:
                out_ref[k * LOCAL : k * LOCAL + LOCAL // 2, :] = own[:, at]
                out_ref[k * LOCAL + LOCAL // 2 : (k + 1) * LOCAL, :] = far[:, at]


def call(body, args, outs, scratch, name, flops, in_bytes, scalars=(), vmem=20):
    return pl.pallas_call(
        body,
        in_specs=[pl.BlockSpec(memory_space=pltpu.SMEM)] * len(scalars)
        + [pl.BlockSpec(memory_space=pltpu.VMEM)] * len(args),
        out_specs=[pl.BlockSpec(memory_space=pltpu.VMEM)] * len(outs),
        out_shape=[jax.ShapeDtypeStruct(shape, dtype) for shape, dtype in outs],
        scratch_shapes=scratch,
        compiler_params=pltpu.CompilerParams(vmem_limit_bytes=vmem * MIB),
        cost_estimate=pl.CostEstimate(flops=flops, bytes_accessed=in_bytes, transcendentals=0),
        name=name,
    )(*scalars, *args)


def back_body(low_ref, g0_ref, g1_ref, w_ref, a_ref, coef_ref, pre_ref, sums_ref, y_ref):
    low = low_ref[0].astype(F32)
    for k in range(9):
        for h, g_ref in enumerate((g0_ref, g1_ref)):
            y_ref[k * LOCAL : (k + 1) * LOCAL, h * HALF : (h + 1) * HALF] = jnp.dot(
                w_ref[k * LOCAL : (k + 1) * LOCAL, :], g_ref[...], preferred_element_type=F32
            )

    def strip(i, carry):
        at = pl.multiple_of(i * 8, 8)
        total = None
        for dc in (-1, 0, 1):
            part = None
            for dr in (-1, 0, 1):
                k = (dr + 1) * 3 + dc + 1
                part = added(part, rows_on(tiles_of(y_ref, k * LOCAL + at, 8), dr, low))
            total = added(total, columns_on(part, dc))
        mean, inv, gain, shift = columns_of(coef_ref[pl.ds(at, 8), :])
        s0, s1 = jnp.zeros((8, 128), F32), jnp.zeros((8, 128), F32)
        for t in range(8):
            a = a_ref[pl.ds(at, 8), t * 128 : (t + 1) * 128].astype(F32)
            normed = (a - mean) * inv
            preact = normed * gain + shift
            gate = jax.nn.sigmoid(preact)
            pre = total[t] * (gate * (1.0 + preact * (1.0 - gate)))
            pre_ref[pl.ds(at, 8), t * 128 : (t + 1) * 128] = pre
            s0, s1 = s0 + pre, s1 + pre * normed
        s0, s1 = jnp.sum(s0, axis=1, keepdims=True), jnp.sum(s1, axis=1, keepdims=True)
        lane = lanes((8, 128))
        sums_ref[pl.ds(at, 8), :] = jnp.where(lane == 0, s0, jnp.where(lane == 1, s1, 0.0))
        return carry

    lax.fori_loop(0, LOCAL // 8, strip, 0, unroll=4)


def back(low, g0, g1, w, a, coef):
    return call(
        back_body,
        (g0, g1, w, a, coef),
        [((LOCAL, PX), F32), ((LOCAL, 128), F32)],
        [pltpu.VMEM((9 * LOCAL, PX), F32)],
        "back",
        2 * 9 * LOCAL * CH * PX,
        5_000_000,
        scalars=(low,),
    )


def prepare_body(low_ref, order_ref, *refs):
    samples, (shifted, plain, ordered) = (refs[:2], refs[2:4]), refs[4:]
    low = low_ref[0].astype(F32)
    for o, (a_ref, coef_ref) in enumerate(samples):

        def activate(i, carry):
            at = pl.multiple_of(i * 16, 16)
            mean, inv, gain, shift = columns_of(coef_ref[pl.ds(at, 16), :])
            for t in range(8):
                a = a_ref[pl.ds(at, 16), t * 128 : (t + 1) * 128].astype(F32)
                preact = (a - mean) * inv * gain + shift
                plain[pl.ds(at, 16), t * 128 : (t + 1) * 128] = (
                    preact * jax.nn.sigmoid(preact)
                ).astype(BF16)
            return carry

        lax.fori_loop(0, LOCAL // 16, activate, 0, unroll=5)
        for p, (taps, _) in enumerate(SCATTER_PARTS):
            ordered[...] = jnp.dot(order_ref[p], plain[...], preferred_element_type=F32)

            def build(i, carry):
                at = pl.multiple_of(i * 16, 16)
                tiles = tiles_of(ordered, at, 16)
                moved = {}
                for k in taps:
                    dr, dc = TAPS[k]
                    if dc not in moved:
                        moved[dc] = columns_on(tiles, -dc)
                    for t, y in enumerate(rows_on(moved[dc], -dr, low)):
                        at_px = o * PX + t * 128
                        row = SEQUENCE.index(k) * LOCAL
                        shifted[pl.ds(row + at, 16), at_px : at_px + 128] = y.astype(BF16)
                return carry

            lax.fori_loop(0, LOCAL // 16, build, 0, unroll=5)


def prepare(low, samples):
    orders = jnp.asarray(np.stack([reorder(o) for _, o in SCATTER_PARTS]), BF16)
    return call(
        prepare_body,
        (orders, *samples[0], *samples[1]),
        [((9 * LOCAL, 2 * PX), BF16)],
        [pltpu.VMEM((LOCAL, PX), BF16), pltpu.VMEM((LOCAL, PX), F32)],
        "prepare",
        2 * 10**9,
        8_000_000,
        scalars=(low,),
    )[0]


def wgrad_body(accumulate, flags_ref, unpick_ref, *refs):
    refs = list(refs)
    outer = [[refs.pop(0) for _ in range(2)] for _ in range(2)]
    slices = [refs.pop(0) for _ in range(4)]
    shifted = refs.pop(0)
    count = 2 * len(SCATTER_PARTS)
    before = [refs.pop(0) for _ in range(count)] if accumulate else None
    outs = [refs.pop(0) for _ in range(count)]
    full = [[refs.pop(0) for _ in range(2)] for _ in range(2)]
    (adjoint,) = refs
    section = flags_ref[1]
    step = pl.program_id(0)

    @pl.when(step == 0)
    def _():
        for o in (0, 1):

            @pl.when(section == 1)
            def _():
                for h in (0, 1):
                    full[o][h][...] = outer[o][h][...]

            @pl.when(section == 0)
            def _():
                for h in (0, 1):
                    total = None
                    for b in range(4):
                        at = (h ^ (b & 1)) * HALF
                        part = jnp.dot(
                            unpick_ref[b],
                            slices[b][o ^ (b >> 1), :, at : at + HALF],
                            preferred_element_type=F32,
                        )
                        total = part if total is None else total + part
                    full[o][h][...] = total.astype(BF16)

            for h in (0, 1):
                at = o * PX + h * HALF
                adjoint[at : at + HALF, :] = full[o][h][...].T

    value = jnp.dot(shifted[...], adjoint[...], preferred_element_type=F32)
    for p, (taps, _) in enumerate(SCATTER_PARTS):
        start = SEQUENCE.index(taps[0])

        @pl.when((step >= start) & (step < start + len(taps)))
        def _():
            for side in (0, 1):
                part = value[side * LOCAL // 2 : (side + 1) * LOCAL // 2]
                if accumulate:
                    part = part + before[2 * p + side][0]
                outs[2 * p + side][0] = part


def wgrad(flags, unpick, outer, slices, shifted, before=()):
    half = LOCAL // 2
    fixed = lambda a: pl.BlockSpec(a.shape, lambda g: (0,) * a.ndim, pipeline_mode=pl.Buffered(1))
    tap_specs, tap_shapes = [], []
    for taps, _ in SCATTER_PARTS:
        start, size = SEQUENCE.index(taps[0]), len(taps)
        for _ in (0, 1):
            tap_specs.append(
                pl.BlockSpec(
                    (1, half, CH),
                    lambda g, start=start, size=size: (jnp.clip(g - start, 0, size - 1), 0, 0),
                )
            )
            tap_shapes.append(jax.ShapeDtypeStruct((size, half, CH), F32))
    args = [unpick, *outer[0], *outer[1], *slices]
    specs = [fixed(a) for a in args] + [pl.BlockSpec((LOCAL, 2 * PX), lambda g: (g, 0))]
    adjoint_spec = pl.BlockSpec((CH, HALF), lambda g: (0, 0))
    got = pl.pallas_call(
        lambda *refs: wgrad_body(bool(before), *refs),
        grid=(9,),
        in_specs=[pl.BlockSpec(memory_space=pltpu.SMEM)] + specs + (tap_specs if before else []),
        out_specs=tap_specs + [adjoint_spec] * 4,
        out_shape=tap_shapes + [jax.ShapeDtypeStruct((CH, HALF), BF16)] * 4,
        scratch_shapes=[pltpu.VMEM((2 * PX, CH), BF16)],
        input_output_aliases={2 + len(args) + i: i for i in range(len(before))},
        compiler_params=pltpu.CompilerParams(vmem_limit_bytes=32 * MIB),
        cost_estimate=pl.CostEstimate(
            flops=2 * 2 * 9 * LOCAL * CH * PX, bytes_accessed=16_000_000, transcendentals=0
        ),
        name="wgrad",
    )(flags, *args, shifted, *before)
    return got[:-4], (got[-4:-2], got[-2:])


def after(x, done):
    return lax.optimization_barrier((x, done))[0]


def merge_body(count, last, *refs):
    for p in range(count):
        total = refs[p][...] + refs[count + p][...]
        if last:
            refs[2 * count + p][...] = total
        else:
            half = total.shape[1] // 2
            refs[2 * count + 2 * p][...] = total[:, :half]
            refs[2 * count + 2 * p + 1][...] = total[:, half:]


def merge(keeps, came, last):
    outs = []
    for k in keeps:
        size, half = k.shape[0], k.shape[1] // 2
        outs += [((size, 2 * half, CH), F32)] if last else [((size, half, CH), F32)] * 2
    count = len(keeps)
    got = call(
        lambda *refs: merge_body(count, last, *refs), (*keeps, *came), outs, [], "merge", 10**6, 4 * 10**6
    )
    return got if last else [tuple(got[2 * p : 2 * p + 2]) for p in range(count)]


def spread(groups):
    return jnp.broadcast_to(groups[..., None], (*groups.shape, SHARD)).reshape(*groups.shape[:-1], LOCAL)


def slots(channels):
    return jnp.sum(channels.reshape(*channels.shape[:-1], 16, SHARD), axis=-1)


def over_four(x):
    x = x + core(x)
    return x + rows(x)


def turn_rows(a):
    return jnp.swapaxes(a.reshape(2, 4, 4, COLS, CH), 1, 2).reshape(2, HALF, CH)


def shards(segment_inputs, weights, gains, shifts, chain_cot, skip_cot):
    count_all = float(PX * CH // GROUPS)
    seg = lax.axis_index("segment")
    dp = lax.axis_index("dp")
    r = lax.axis_index("rows")
    c = dp % 2
    me = dp // 2
    low = jnp.stack([r, seg]).astype(jnp.int32)

    mine = lax.dynamic_slice_in_dim(weights[0], r * SHARD, SHARD, axis=1)
    gathered = [
        jnp.transpose(mine[taps[0] : taps[-1] + 1], (1, 0, 2)).reshape(SHARD, -1)
        for taps, _ in GATHER_PARTS
    ]
    for stage in (3, 2, 1):
        came = [chip(cur, ORDERS[order][stage]) for cur, (_, order) in zip(gathered, GATHER_PARTS)]
        gathered = [jnp.concatenate([cur, other], axis=0) for cur, other in zip(gathered, came)]
        if stage == 2:
            early = gathered
    weight_parts = []
    for cur, (_, order) in zip(gathered, GATHER_PARTS):
        weight_parts += [cur, chip(cur, ORDERS[order][0])]
    fix = jnp.asarray(reorder(GATHER_PARTS[1][1]).T, BF16)

    row = np.arange(CH)
    flips = np.asarray(slot_masks(ORDERS[0]))[row // SHARD % 16]
    natural = (
        40 * (me ^ jnp.asarray(flips, jnp.int32))
        + 20 * (c ^ jnp.asarray(row // 320, jnp.int32))
        + 10 * (r ^ jnp.asarray(row // LOCAL % 2, jnp.int32))
        + jnp.asarray(row % SHARD, jnp.int32)
    )
    hit = natural[:, None] == lax.broadcasted_iota(jnp.int32, (CH, CH), 1)
    pick = hit.astype(BF16)
    own_hit = hit[:LOCAL]
    eye = jnp.eye(CH, dtype=BF16)
    column = natural.reshape(4, 1, LOCAL)
    unpick = (column == lax.broadcasted_iota(jnp.int32, (4, CH, LOCAL), 1)).astype(BF16)

    total = chain_cot.astype(F32) + skip_cot.astype(F32)
    flat = turn_rows(total.astype(BF16))
    outer_t = jnp.einsum("ij,npj->nip", eye, flat, preferred_element_type=F32).astype(BF16)
    outer = []
    for n in range(2):
        near = outer_t[n]
        far = along_z(near, [(2, 3), (3, 2)] if n == 0 else [(1, 2), (0, 3)])
        outer.append(((near, far), (core(near), core(far))))

    local = turn_rows(after(segment_inputs[0], early))
    picked = jnp.einsum("ij,npj->nip", pick, local, preferred_element_type=F32).astype(BF16)
    wide = picked.astype(F32)
    stats = jnp.stack([jnp.sum(wide, -1), jnp.sum(wide * wide, -1)], axis=1)
    stats = jnp.sum(stats.reshape(2, 2, 4, 16, SHARD), axis=(2, 4))
    stats = stats + rows(stats)
    stats = jnp.stack([stats, core(stats)], axis=1)
    mean = stats[:, :, 0] / count_all
    inv = lax.rsqrt(stats[:, :, 1] / count_all - mean * mean + epsilon)
    picked = picked.reshape(2, 2, 2, LOCAL, HALF)
    both = jnp.concatenate([picked[:, :, 0], rows(picked[:, :, 1])], axis=-1)
    theirs = core(both[:, 1])
    inputs = [(both[n, 0], theirs[n]) for n in range(2)]

    gain = jnp.sum(jnp.where(own_hit, gains[0][None, :], 0.0), axis=1)
    shift = jnp.sum(jnp.where(own_hit, shifts[0][None, :], 0.0), axis=1)
    mean_c, inv_c = spread(mean), spread(inv)
    coef = jnp.stack(
        [mean_c, inv_c, jnp.broadcast_to(gain, mean_c.shape), jnp.broadcast_to(shift, mean_c.shape)],
        axis=-1,
    )
    coef = jnp.pad(coef, ((0, 0), (0, 0), (0, 0), (0, 124)))

    (w,) = call(
        assemble_body, (fix, *weight_parts), [((9 * LOCAL, CH), BF16)], [], "assemble", 10**8, 4_000_000
    )

    def in_grads(halves, gate=None, totals=False):
        pres, parts = [], []
        for n in range(2):
            for o in range(2):
                pre, part = back(low, *halves[n][o], w, inputs[n][o], coef[n, o])
                pres.append(pre)
                parts.append(part[:, :2])
        s = jnp.stack(parts)
        packed = slots(jnp.moveaxis(s * gain[None, :, None], 2, 1)).reshape(128)
        if totals:
            s = jnp.sum(s, axis=0)
            placed = jnp.sum(jnp.where(own_hit[:, None, :], s[:, :, None], 0.0), axis=0)
            packed = jnp.concatenate([packed, placed.reshape(2 * CH)])
        if gate is not None:
            packed = after(packed, gate)
        came = core(packed)
        came = [came[32:64], came[:32], came[96:128], came[64:96], came[128:]]
        packed = packed + jnp.concatenate(came)
        packed = packed + rows(packed)
        group = packed[:128].reshape(2, 2, 2, 16)
        grads = []
        for n in range(2):
            grads.append([])
            for o in range(2):
                first = spread(group[n, o, 0] / count_all)[:, None]
                second = spread(group[n, o, 1] / count_all)[:, None]
                normed = (inputs[n][o].astype(F32) - mean_c[n, o][:, None]) * inv_c[n, o][:, None]
                grads[n].append(
                    inv_c[n, o][:, None] * (pres[2 * n + o] * gain[:, None] - first - normed * second)
                )
        return grads, packed[128:]

    grads, _ = in_grads(outer)
    handed = [jnp.stack(grads[n]).astype(BF16) for n in range(2)]
    ready = after(coef, handed)
    shifted = [prepare(low, [(inputs[n][o], ready[n, o]) for o in range(2)]) for n in range(2)]
    slices, hops = [], None
    for n in range(2):
        pair = handed[n] if hops is None else after(handed[n], hops)
        hops = along_z(pair, [(2, 1), (3, 0)])
        if n == 0:
            hops = after(hops, shifted)
        two = along_z(hops, [(0, 1), (1, 0)])
        slices.append((two, hops, core(hops)))

    def returned(n, grads):
        split = []
        for o in range(2):
            high = lax.reduce_precision(grads[o], 8, 7)
            split.append(jnp.stack([high, grads[o] - high]).astype(BF16))
        two = jnp.stack([split[0], core(split[1])], axis=1)
        arrived = rows(two[..., HALF:])
        two = jnp.stack([two[..., :HALF], arrived], axis=2).reshape(2, CH, HALF)
        nat = jnp.einsum("tjp,ji->tpi", two, pick, preferred_element_type=F32)
        nat = jnp.swapaxes(nat.reshape(2, 4, 4, COLS, CH), 1, 2).reshape(2, HALF // COLS, COLS, CH)
        wide = chain_cot[n].astype(F32) + skip_cot[n].astype(F32)
        return (nat[0] + jnp.where(seg == 0, nat[1] + wide, 0.0)).astype(BF16), arrived

    two, one, across = slices[0]
    weight_grads, full = wgrad(low, unpick, outer[0], (two, one, core(two), across), shifted[0])
    two, one, across = slices[1]
    two = after(two, weight_grads)
    weight_grads, last_full = wgrad(
        low, unpick, outer[1], (two, one, core(two), across), shifted[1], weight_grads
    )
    full = after(full, weight_grads)

    sides = [weight_grads[2 * p : 2 * p + 2] for p in range(len(SCATTER_PARTS))]
    for stage in range(4):
        came = [chip(give, ORDERS[order][stage]) for (_, give), (_, order) in zip(sides, SCATTER_PARTS)]
        came = lax.optimization_barrier(came)
        if stage == 0:
            grads, norm_sums = in_grads((full, last_full), came, True)
        if stage > 1:
            norm_sums = after(norm_sums, came)
            norm_sums = norm_sums + chip(norm_sums, ORDERS[0][stage - 2])
        sides = merge([keep for keep, _ in sides], came, stage == 3)
    now = sides
    results = [returned(n, grads[n])[0] for n in range(2)]
    outputs = jnp.stack(results)[None]
    for mask in ORDERS[0][2:]:
        norm_sums = norm_sums + chip(norm_sums, mask)
    norm_sums = norm_sums.reshape(2, CH)
    shard = jnp.concatenate(now, axis=0)
    shard = jnp.stack([shard[SEQUENCE.index(k)] for k in range(9)])
    far_shard = rows(shard)
    weight_grad = jnp.where(
        r == 0,
        jnp.concatenate([shard, far_shard], axis=1),
        jnp.concatenate([far_shard, shard], axis=1),
    )
    return (outputs, weight_grad[None], norm_sums[1][None], norm_sums[0][None])


def solution(mesh):
    placed = (
        P("segment", "dp", "rows", None, None),
        P("segment", None, "dp", None),
        P("segment", None),
        P("segment", None),
        P("dp", "rows", None, None),
        P("dp", "rows", None, None),
    )
    return jax.shard_map(
        shards,
        mesh=mesh,
        in_specs=placed,
        out_specs=(
            P("segment", "dp", "rows", None, None),
            P("segment", None, "dp", None),
            P("segment", None),
            P("segment", None),
        ),
        check_vma=False,
    )
```
